32 devices in a mesh: tm: 8 (over z, core), trace: 4 (over y, x).
Axes of the slice: x: 2, y: 2, z: 4, core: 2. Of those that a mesh axis runs over, the one named last changes fastest.
Arguments:
- observed: bfloat16 [64, 4096], P('trace', 'tm'), may hold values from -32 to 32
- sampled: int32 [64, 4096], P('trace', 'tm'), may hold values 0 or 1
- probes: bfloat16 [256, 64, 128], P(None, 'trace'), may hold values from -0.046875 to 0.046875
Outputs:
- completed: float32 [64, 4096], P('trace', 'tm')
The draws below stay inside these ranges and needn't reach their ends.
All inputs are finite; a program needn't handle non-finite values. No bound on the sum of `sampled` on one device may be relied on, other than what follows from the above.
Results may differ from the reference program's by a relative error of at most 0.0004.
Values may be sent and summed in bfloat16 or wider, within the bound.
A program may use at most 64 MiB of HBM per device.

```python
import jax
import jax.numpy as jnp
from jax import lax

TAPS = 256
PROBES = 128
TRACES = 64
SAMPLES = 4096


def draw_observed(key, part):
    keys = jax.random.split(jax.random.fold_in(key, 11), 7)
    count = PROBES
    omega = jax.random.uniform(keys[0], (count,), minval=0.05, maxval=2.5)
    kappa = jax.random.uniform(keys[1], (count,), minval=-1.2, maxval=1.2)
    phase = jax.random.uniform(keys[2], (count,), minval=-3.14159, maxval=3.14159)
    amplitude = jnp.exp(jax.random.uniform(keys[3], (count,), minval=-1.2, maxval=0.4)) * (2.0 / count) ** 0.5
    times = jnp.arange(SAMPLES, dtype=jnp.float32)
    traces = jnp.arange(TRACES, dtype=jnp.float32)

    def add_wave(total, index):
        wave = amplitude[index] * jnp.cos(omega[index] * times[None, :] + kappa[index] * traces[:, None] + phase[index])
        return (total + wave, None)
    signal, unused = lax.scan(add_wave, jnp.zeros((TRACES, SAMPLES), jnp.float32), jnp.arange(count))
    noise = 0.3 * jax.random.normal(keys[4], (TRACES, SAMPLES))
    segment = jnp.exp(jax.random.uniform(keys[5], (SAMPLES // 16,), minval=-0.693, maxval=0.693))
    time_gain = jnp.repeat(segment, 16) * (1.0 + 2.0 * times / SAMPLES)
    trace_gain = jnp.exp(jax.random.uniform(keys[6], (TRACES,), minval=-0.357, maxval=0.336)) * (1.0 + 2.0 * traces / TRACES)
    values = (signal + noise) * time_gain[None, :] * trace_gain[:, None] / 3.0
    return jnp.clip(values, -32.0, 32.0).astype(jnp.bfloat16)


def touch_ends(result, stream_key, low, largest):
    index_at = [jax.random.randint(jax.random.fold_in(stream_key, axis), (), 0, length) for axis, length in enumerate(result.shape)]
    main_axis = result.shape.index(max(result.shape))
    next_to = index_at[:main_axis] + [(index_at[main_axis] + 1) % result.shape[main_axis]] + index_at[main_axis + 1:]
    return result.at[tuple(index_at)].set(low).at[tuple(next_to)].set(largest)


def block_scale(rng, shape, shards, smallest, top_value):
    factor_of = 1.0
    for dim, parts in shards:
        steps = jax.random.uniform(jax.random.fold_in(jax.random.fold_in(rng, 6), dim), (parts,), jnp.float32, smallest / len(shards), top_value / len(shards))
        factor_of = factor_of * jnp.repeat(jnp.exp(steps), shape[dim] // parts).reshape((-1,) + (1,) * (len(shape) - 1 - dim))
    return factor_of


def gaussian(rng, shape, deviation, reach, cuts=(), kind=jnp.bfloat16):
    entries = deviation * jax.random.normal(rng, shape, jnp.float32)
    if cuts:
        entries = entries * block_scale(rng, shape, cuts, -0.22, 0.18)
    return jnp.clip(entries, -reach, reach).astype(kind)


def setup_inputs(seed: int = 0) -> dict:
    streams_of = jax.random.split(jax.random.key(seed), 4)
    return {
        "observed": draw_observed(jax.random.fold_in(streams_of[3], 71), 0),
        "sampled": touch_ends((jax.random.randint(streams_of[1], (TRACES, SAMPLES), 0, 3) < 2).astype(jnp.int32), jax.random.fold_in(streams_of[1], 1), 0, 1),
        "probes": gaussian(streams_of[2], (TAPS, TRACES, PROBES), (TAPS * TRACES) ** -0.5, 0.046875, ((1, 4),)),
    }


def correlate(signal, kernel, numbers):
    return lax.conv_general_dilated(signal, kernel, (1,), 'VALID', dimension_numbers=numbers, preferred_element_type=jnp.float32)

def reference(observed, sampled, probes):
    taps = probes.shape[0]
    data = jnp.where(sampled == 1, observed, jnp.zeros_like(observed))
    extended = jnp.pad(data, ((0, 0), (0, taps - 1)))
    sketch = correlate(extended[None], probes, ('NCW', 'WIO', 'NWC'))[0]
    gram = jnp.dot(sketch.T.astype(jnp.float32), sketch.astype(jnp.float32), precision=lax.Precision.HIGHEST, preferred_element_type=jnp.float32)
    lower = jnp.linalg.cholesky(gram)
    basis = lax.linalg.triangular_solve(lower, sketch, left_side=False, lower=True, transpose_a=True).astype(jnp.bfloat16)
    coefs = correlate(extended[:, None, :], basis[:, None, :], ('NCW', 'WIO', 'NWC')).astype(jnp.bfloat16)
    kernel = jnp.flip(jnp.transpose(coefs, (1, 2, 0)), 0)
    padded = jnp.pad(basis, ((taps - 1, 0), (0, 0)))
    summed = correlate(padded[None], kernel, ('NWC', 'WIO', 'NCW'))[0]
    counts = jnp.minimum(jnp.arange(SAMPLES, dtype=jnp.int32) + 1, taps).astype(jnp.float32)
    estimate = summed / counts[None, :]
    return jnp.where(sampled == 1, observed.astype(jnp.float32), estimate)
```

```python
import functools

import jax
import jax.numpy as jnp
from jax import lax
from jax.experimental import pallas as pl
from jax.experimental.pallas import tpu as pltpu
from jax.sharding import PartitionSpec as P

LANES = 128
SUB = 8
BF = jnp.bfloat16
F32 = jnp.float32


def nt(a, b):
    return lax.dot_general(a, b, (((1,), (1,)), ((), ())), preferred_element_type=F32)


def nn(a, b):
    return lax.dot_general(a, b, (((1,), (0,)), ((), ())), preferred_element_type=F32)


def split3(x):
    hi = x.astype(BF)
    rest = x - hi.astype(F32)
    mid = rest.astype(BF)
    low = (rest - mid.astype(F32)).astype(BF)
    return hi, mid, low


def inverse_factor(gram):
    size = gram.shape[0]
    blocks = size // SUB
    rows = lax.broadcasted_iota(jnp.int32, (SUB, size), 0)
    lanes = lax.broadcasted_iota(jnp.int32, (SUB, size), 1)
    left = [gram[SUB * a : SUB * (a + 1)] for a in range(blocks)]
    right = [jnp.where(lanes == rows + SUB * a, 1.0, 0.0).astype(F32) for a in range(blocks)]
    scales = []
    for a0 in range(blocks):
        wide = {
            a: [jnp.broadcast_to(left[a][:, SUB * a0 + q : SUB * a0 + q + 1], (SUB, size)) for q in range(SUB)]
            for a in range(a0, blocks)
        }
        scale = jnp.zeros((SUB, size), F32)
        for s in range(SUB):
            pivot = wide[a0][s][s : s + 1]
            inverse = 1.0 / pivot
            scale = jnp.where(rows == s, pivot, scale)
            row_left = left[a0][s : s + 1] * inverse
            row_right = right[a0][s : s + 1] * inverse
            row_wide = {q: wide[a0][q][s : s + 1] * inverse for q in range(s + 1, SUB)}
            for a in range(a0, blocks):
                factor = wide[a][s]
                if a == a0:
                    factor = jnp.where(rows > s, factor, 0.0)
                left[a] = left[a] - factor * row_left
                right[a] = right[a] - factor * row_right
                for q in range(s + 1, SUB):
                    wide[a][q] = wide[a][q] - factor * row_wide[q]
        scales.append(lax.rsqrt(scale))
    return jnp.concatenate([right[a] * scales[a] for a in range(blocks)], axis=0)


def kernel(
    n_tm, n_tr,
    observed, sampled, probes, out,
    data, halo, slices, windows, rolled, probes_t, part, parts_in, sketch, flat,
    hankel, spread, est_out, est_in,
    halo_sems, win_send, win_recv, part_send, part_recv,
    z_send, z_recv, x_send, x_recv, c_send, c_recv, est_send, est_recv,
):
    tm = lax.axis_index("tm")
    tr = lax.axis_index("trace")
    n_z = n_tm // 2
    z = tm // 2
    core = lax.rem(tm, 2)
    traces, width = data.shape
    own = traces // n_tm
    groups, contract, probe_count = probes.shape
    taps = groups * LANES
    chunks = width // LANES
    total = n_tm * chunks
    samples = n_tm * width
    share = part.shape[0] // n_tr

    def copy(src, dst, send, recv, **to):
        return pltpu.make_async_remote_copy(
            src_ref=src, dst_ref=dst, send_sem=send, recv_sem=recv,
            device_id=to, device_id_type=pl.DeviceIdType.MESH,
        )

    barrier = pltpu.get_barrier_semaphore()
    for off in range(1, n_tm):
        pl.semaphore_signal(barrier, inc=1, device_id={"tm": lax.rem(tm + off, n_tm)}, device_id_type=pl.DeviceIdType.MESH)
    for off in range(1, n_tr):
        pl.semaphore_signal(barrier, inc=1, device_id={"trace": lax.rem(tr + off, n_tr)}, device_id_type=pl.DeviceIdType.MESH)

    masked = jnp.where(sampled[...] == 1, observed[...].astype(F32), 0.0)
    data[...] = masked.astype(BF)
    for i in range(n_tm):
        slices[i] = masked[own * i : own * (i + 1)]
    pl.semaphore_wait(barrier, n_tm + n_tr - 2)

    pending = []
    before = lax.rem(tm + n_tm - 1, n_tm)
    halo_copy = copy(data.at[:, pl.ds(0, taps)], halo, halo_sems.at[0], halo_sems.at[1], tm=before)
    halo_copy.start()
    pending.append(halo_copy)
    for off in range(1, n_tm):
        dst = lax.rem(tm + off, n_tm)
        c = copy(slices.at[dst], windows.at[tm], win_send.at[off], win_recv.at[off], tm=dst)
        c.start()
        pending.append(c)
    windows[tm] = slices[tm]

    with jax.named_scope("probes_transposed"):
        for g in range(groups):
            probes_t[probe_count * g : probe_count * (g + 1), :] = probes[g].T

    halo_copy.wait_recv()
    with jax.named_scope("sketch_part"):
        tail = jnp.where(tm < n_tm - 1, halo[...].astype(F32), 0.0)
        extended = jnp.concatenate([masked, tail], axis=1)
        reach = extended.shape[1]
        keep = rolled.shape[1]
        for j in range(LANES):
            moved = pltpu.roll(extended, reach - j, 1) if j else extended
            rolled[traces * j : traces * (j + 1), :] = moved[:, :keep].astype(BF)
        both = nn(probes_t[...], rolled[...])
        for b in range(chunks):
            block = both[:probe_count, LANES * b : LANES * (b + 1)]
            for g in range(1, groups):
                block = block + both[probe_count * g : probe_count * (g + 1), LANES * (b + g) : LANES * (b + g + 1)]
            part[probe_count * b : probe_count * (b + 1), :] = block.astype(BF)

    part_copies = []
    for off in range(1, n_tr):
        dst = lax.rem(tr + off, n_tr)
        c = copy(
            part.at[pl.ds(pl.multiple_of(dst * share, share), share), :], parts_in.at[tr],
            part_send.at[off], part_recv.at[off], trace=dst,
        )
        c.start()
        pending.append(c)
    summed = part[pl.ds(pl.multiple_of(tr * share, share), share), :].astype(F32)
    for off in range(1, n_tr):
        src = lax.rem(tr + n_tr - off, n_tr)
        copy(
            part.at[pl.ds(0, share), :], parts_in.at[src], part_send.at[off], part_recv.at[off], trace=src
        ).wait_recv()
        summed = summed + parts_in[src].astype(F32)
    sketch[tm, pl.ds(pl.multiple_of(tr * share, share), share), :] = summed.astype(BF)

    def place(zo, ro, parity):
        t = lax.rem(z + n_z - zo, n_z) * 2 + parity
        r = lax.rem(tr + n_tr - ro, n_tr)
        return sketch.at[t, pl.ds(pl.multiple_of(r * share, share), share), :]

    def along_z(zo):
        here = place(0, 0, core)
        return copy(here, here, z_send.at[zo], z_recv.at[zo], tm=lax.rem(z + zo, n_z) * 2 + core)

    def across(zo, ro):
        here = place(zo, 0, core)
        return copy(here, here, x_send.at[zo, ro], x_recv.at[zo, ro], trace=lax.rem(tr + ro, n_tr))

    def to_sibling(zo, ro):
        here = place(zo, ro, core)
        return copy(here, here, c_send.at[zo, ro], c_recv.at[zo, ro], tm=z * 2 + 1 - core)

    def go(c):
        c.start()
        pending.append(c)

    def arrived(zo, ro, send, recv, parity):
        there = place(zo, ro, parity)
        copy(there, there, send, recv, tm=z * 2 + 1 - core).wait_recv()

    for zo in range(1, n_z):
        go(along_z(zo))
    for ro in range(1, n_tr):
        go(across(0, ro))
    go(to_sibling(0, 0))

    for off in range(1, n_tm):
        src = lax.rem(tm + n_tm - off, n_tm)
        copy(slices.at[src], windows.at[src], win_send.at[off], win_recv.at[off], tm=src).wait_recv()
    with jax.named_scope("hankel"):
        rows = lax.broadcasted_iota(jnp.int32, (LANES, LANES), 0)
        lanes = lax.broadcasted_iota(jnp.int32, (LANES, LANES), 1)
        for c in range(own):
            ahead = None
            for m in range(total + groups - 2, -1, -1):
                if m < total:
                    t, b = m // chunks, m % chunks
                    line = windows[t, c : c + 1, LANES * b : LANES * (b + 1)]
                    now = pltpu.roll(jnp.broadcast_to(line, (LANES, LANES)), 1, 1, stride=1, stride_axis=0)
                else:
                    now = jnp.zeros((LANES, LANES), F32)
                if ahead is None:
                    ahead = jnp.zeros((LANES, LANES), F32)
                hankel[LANES * c : LANES * (c + 1), LANES * m : LANES * (m + 1)] = jnp.where(
                    lanes <= rows, now, ahead
                ).astype(BF)
                ahead = now

    for zo in range(1, n_z):
        arrived(zo, 0, z_send.at[zo], z_recv.at[zo], core)
        for ro in range(1, n_tr):
            go(across(zo, ro))
        go(to_sibling(zo, 0))
    for zo in range(n_z):
        for ro in range(1, n_tr):
            arrived(zo, ro, x_send.at[zo, ro], x_recv.at[zo, ro], core)
            go(to_sibling(zo, ro))
    for zo in range(n_z):
        for ro in range(n_tr):
            arrived(zo, ro, c_send.at[zo, ro], c_recv.at[zo, ro], 1 - core)

    with jax.named_scope("gram"):
        for t in range(n_tm):
            for b in range(chunks):
                m = t * chunks + b
                flat[:, LANES * m : LANES * (m + 1)] = sketch[t, probe_count * b : probe_count * (b + 1), :]
        gram = nt(flat[...], flat[...])
    with jax.named_scope("inverse_factor"):
        hi, mid, low = split3(inverse_factor(gram))
    with jax.named_scope("basis"):
        for g in range(groups):
            rows_g = slice(probe_count * g, probe_count * (g + 1))
            if g:
                spread[rows_g, : LANES * g] = jnp.zeros((probe_count, LANES * g), BF)
            if g < groups - 1:
                spread[rows_g, LANES * (total + g) :] = jnp.zeros((probe_count, LANES * (groups - 1 - g)), BF)
        for t in range(n_tm):
            piece = flat[:, width * t : width * (t + 1)]
            basis = (nn(low, piece) + nn(mid, piece) + nn(hi, piece)).astype(BF)
            for g in range(groups):
                spread[probe_count * g : probe_count * (g + 1), width * t + LANES * g : width * (t + 1) + LANES * g] = basis
    with jax.named_scope("coefs"):
        coefs = nt(hankel[...], spread[...]).astype(BF)
        flip = jnp.where(lanes + rows == LANES - 1, 1.0, 0.0).astype(BF)
        coefs = jnp.concatenate(
            [nn(flip, coefs[LANES * c : LANES * (c + 1)]).astype(BF) for c in range(own)], axis=0
        )
    with jax.named_scope("antidiagonals"):
        carry = [jnp.zeros((SUB, LANES), F32) for _ in range(own)]
        for t in range(n_tm):
            product = nn(coefs, spread[:, width * t : width * (t + 1)])
            for c in range(own):
                for b in range(chunks):
                    block = product[LANES * c : LANES * (c + 1), LANES * b : LANES * (b + 1)]
                    turned = pltpu.roll(block, 0, 1, stride=1, stride_axis=0)
                    inside = jnp.where(lanes >= rows, turned, 0.0)
                    beyond = turned - inside
                    near = carry[c]
                    far = jnp.zeros((SUB, LANES), F32)
                    for a in range(LANES // SUB):
                        near = near + inside[SUB * a : SUB * (a + 1)]
                        far = far + beyond[SUB * a : SUB * (a + 1)]
                    carry[c] = far
                    est_out[t, c : c + 1, LANES * b : LANES * (b + 1)] = jnp.sum(near, axis=0, keepdims=True)

    for off in range(1, n_tm):
        dst = lax.rem(tm + off, n_tm)
        go(copy(est_out.at[dst], est_in.at[tm], est_send.at[off], est_recv.at[off], tm=dst))
    est_in[tm] = est_out[tm]
    for off in range(1, n_tm):
        src = lax.rem(tm + n_tm - off, n_tm)
        copy(est_out.at[src], est_in.at[src], est_send.at[off], est_recv.at[off], tm=src).wait_recv()
    estimate = jnp.concatenate([est_in[i] for i in range(n_tm)], axis=0)
    position = tm * width + lax.broadcasted_iota(jnp.int32, (traces, width), 1)
    counts = jnp.minimum(position + 1, taps).astype(F32)
    out[...] = jnp.where(sampled[...] == 1, observed[...].astype(F32), estimate / counts)
    for c in pending:
        c.wait_send()


def on_device(observed, sampled, probes):
    n_tm, n_tr = lax.axis_size("tm"), lax.axis_size("trace")
    taps, traces, count = probes.shape
    width = observed.shape[1]
    groups = taps // LANES
    chunks = width // LANES
    total = n_tm * chunks
    own = traces // n_tm
    n_z = n_tm // 2
    probes = probes.reshape(groups, LANES * traces, count)
    vmem = pl.BlockSpec(memory_space=pltpu.VMEM)
    dma = pltpu.SemaphoreType.DMA
    return pl.pallas_call(
        functools.partial(kernel, n_tm, n_tr),
        out_shape=jax.ShapeDtypeStruct((traces, width), F32),
        in_specs=[vmem] * 3,
        out_specs=vmem,
        scratch_shapes=[
            pltpu.VMEM((traces, width), BF),
            pltpu.VMEM((traces, taps), BF),
            pltpu.VMEM((n_tm, own, width), F32),
            pltpu.VMEM((n_tm, own, width), F32),
            pltpu.VMEM((LANES * traces, width + taps - LANES), BF),
            pltpu.VMEM((groups * count, LANES * traces), BF),
            pltpu.VMEM((chunks * count, LANES), BF),
            pltpu.VMEM((n_tr, chunks * count // n_tr, LANES), BF),
            pltpu.VMEM((n_tm, chunks * count, LANES), BF),
            pltpu.VMEM((count, n_tm * width), BF),
            pltpu.VMEM((own * LANES, (total + groups - 1) * LANES), BF),
            pltpu.VMEM((groups * count, (total + groups - 1) * LANES), BF),
            pltpu.VMEM((n_tm, own, width), F32),
            pltpu.VMEM((n_tm, own, width), F32),
            dma((2,)),
            dma((n_tm,)), dma((n_tm,)),
            dma((n_tr,)), dma((n_tr,)),
            dma((n_z,)), dma((n_z,)),
            dma((n_z, n_tr)), dma((n_z, n_tr)),
            dma((n_z, n_tr)), dma((n_z, n_tr)),
            dma((n_tm,)), dma((n_tm,)),
        ],
        compiler_params=pltpu.CompilerParams(
            collective_id=0, has_side_effects=True, vmem_limit_bytes=56 * 1024 * 1024
        ),
        cost_estimate=pl.CostEstimate(flops=2 * 10**9, bytes_accessed=2 * 10**6, transcendentals=0),
    )(observed, sampled, probes)


def solution(mesh):
    in_specs = (P("trace", "tm"), P("trace", "tm"), P(None, "trace", None))
    out_specs = P("trace", "tm")
    return jax.shard_map(
        on_device, mesh=mesh, in_specs=in_specs, out_specs=out_specs, check_vma=False
    )
```

```python
import functools

import jax
import jax.numpy as jnp
from jax import lax
from jax.experimental import pallas as pl
from jax.experimental.pallas import tpu as pltpu
from jax.sharding import PartitionSpec as P

LANES = 128
SUB = 8
BF = jnp.bfloat16
F32 = jnp.float32


def nt(a, b):
    return lax.dot_general(a, b, (((1,), (1,)), ((), ())), preferred_element_type=F32)


def nn(a, b):
    return lax.dot_general(a, b, (((1,), (0,)), ((), ())), preferred_element_type=F32)


def split3(x):
    hi = x.astype(BF)
    rest = x - hi.astype(F32)
    mid = rest.astype(BF)
    low = (rest - mid.astype(F32)).astype(BF)
    return hi, mid, low


def inverse_factor(gram):
    size = gram.shape[0]
    blocks = size // SUB
    full_rows = lax.broadcasted_iota(jnp.int32, (size, size), 0)
    full_lanes = lax.broadcasted_iota(jnp.int32, (size, size), 1)
    diagonal = jnp.where(full_rows == full_lanes, gram, 0.0)
    by_row = lax.rsqrt(jnp.sum(diagonal, axis=1, keepdims=True))
    by_lane = lax.rsqrt(jnp.sum(diagonal, axis=0, keepdims=True))
    gram = gram * by_row * by_lane
    rows = lax.broadcasted_iota(jnp.int32, (SUB, size), 0)
    lanes = lax.broadcasted_iota(jnp.int32, (SUB, size), 1)
    left = [gram[SUB * a : SUB * (a + 1)] for a in range(blocks)]
    right = [jnp.where(lanes == rows + SUB * a, 1.0, 0.0).astype(F32) for a in range(blocks)]
    found = []

    def at(x, s):
        return jnp.broadcast_to(x[s : s + 1], (SUB, size))

    for a0 in range(blocks):
        columns = {
            a: [jnp.broadcast_to(left[a][:, SUB * a0 + q : SUB * a0 + q + 1], (SUB, size)) for q in range(SUB)]
            for a in range(a0, blocks)
        }
        wide = columns.pop(a0)
        panel = {"left": left[a0], "right": right[a0]}
        taken = jnp.zeros((SUB, size), F32)
        scale = jnp.ones((SUB, size), F32)
        for s in range(0, SUB, 2):
            first, second = wide[s], wide[s + 1]
            p, q, r = at(first, s), at(first, s + 1), at(second, s + 1)
            det = p * r - q * q
            inverse = 1.0 / det
            here = (rows == s) | (rows == s + 1)
            f0, f1 = jnp.where(here, 0.0, first), jnp.where(here, 0.0, second)

            def eliminate(x):
                x0, x1 = at(x, s), at(x, s + 1)
                y0 = (r * x0 - q * x1) * inverse
                y1 = (p * x1 - q * x0) * inverse
                rest = jnp.where(rows == s, y0, jnp.where(rows == s + 1, y1, x))
                return rest - (f0 * y0 + f1 * y1)

            x0, x1 = at(panel["right"], s), at(panel["right"], s + 1)
            taken = jnp.where(rows == s, x0, jnp.where(rows == s + 1, x1 - (q / p) * x0, taken))
            scale = jnp.where(rows == s, p, jnp.where(rows == s + 1, det / p, scale))
            for k in range(s + 2, SUB):
                wide[k] = eliminate(wide[k])
            panel = {side: eliminate(x) for side, x in panel.items()}
        found.append(taken * lax.rsqrt(scale))
        solved_left = [at(panel["left"], s) for s in range(SUB)]
        solved_right = [at(panel["right"], s) for s in range(SUB)]
        for a in range(a0 + 1, blocks):
            for q in range(SUB):
                left[a] = left[a] - columns[a][q] * solved_left[q]
                right[a] = right[a] - columns[a][q] * solved_right[q]
    return jnp.concatenate(found, axis=0) * by_lane


def kernel(
    n_tm, n_tr,
    observed, sampled, probes_in, out,
    probes, probes_sem, data, halo, slices, windows, rolled, probes_t, part, parts_in, sketch, flat,
    hankel, spread, est_out, est_in,
    halo_sems, win_send, win_recv, part_send, part_recv,
    z_send, z_recv, x_send, x_recv, c_send, c_recv, est_send, est_recv,
):
    tm = lax.axis_index("tm")
    tr = lax.axis_index("trace")
    n_z = n_tm // 2
    z = tm // 2
    core = lax.rem(tm, 2)
    traces, width = data.shape
    own = traces // n_tm
    groups, contract, probe_count = probes.shape
    fetch = pltpu.make_async_copy(probes_in, probes, probes_sem)
    fetch.start()
    taps = groups * LANES
    chunks = width // LANES
    total = n_tm * chunks
    samples = n_tm * width
    share = part.shape[0] // n_tr

    def copy(src, dst, send, recv, **to):
        return pltpu.make_async_remote_copy(
            src_ref=src, dst_ref=dst, send_sem=send, recv_sem=recv,
            device_id=to, device_id_type=pl.DeviceIdType.MESH,
        )

    barrier = pltpu.get_barrier_semaphore()
    for off in range(1, n_tm):
        pl.semaphore_signal(barrier, inc=1, device_id={"tm": lax.rem(tm + off, n_tm)}, device_id_type=pl.DeviceIdType.MESH)
    for off in range(1, n_tr):
        pl.semaphore_signal(barrier, inc=1, device_id={"trace": lax.rem(tr + off, n_tr)}, device_id_type=pl.DeviceIdType.MESH)

    masked = jnp.where(sampled[...] == 1, observed[...].astype(F32), 0.0)
    data[...] = masked.astype(BF)
    for i in range(n_tm):
        slices[i] = masked[own * i : own * (i + 1)]
    pl.semaphore_wait(barrier, n_tm + n_tr - 2)

    pending = []
    before = lax.rem(tm + n_tm - 1, n_tm)
    halo_copy = copy(data.at[:, pl.ds(0, taps)], halo, halo_sems.at[0], halo_sems.at[1], tm=before)
    halo_copy.start()
    pending.append(halo_copy)
    for off in range(1, n_tm):
        dst = lax.rem(tm + off, n_tm)
        c = copy(slices.at[dst], windows.at[tm], win_send.at[off], win_recv.at[off], tm=dst)
        c.start()
        pending.append(c)
    windows[tm] = slices[tm]

    fetch.wait()
    with jax.named_scope("probes_transposed"):
        for g in range(groups):
            probes_t[probe_count * g : probe_count * (g + 1), :] = probes[g].T

    halo_copy.wait_recv()
    with jax.named_scope("sketch_part"):
        tail = jnp.where(tm < n_tm - 1, halo[...].astype(F32), 0.0)
        extended = jnp.concatenate([masked, tail], axis=1)
        reach = extended.shape[1]
        keep = rolled.shape[1]
        both = jnp.zeros((groups * probe_count, keep), F32)
        step = LANES // 4
        for first in range(0, LANES, step):
            for j in range(first, first + step):
                moved = pltpu.roll(extended, reach - j, 1) if j else extended
                rolled[traces * j : traces * (j + 1), :] = moved[:, :keep].astype(BF)
            some = slice(traces * first, traces * (first + step))
            both = both + nn(probes_t[:, some], rolled[some, :])
        for b in range(chunks):
            block = both[:probe_count, LANES * b : LANES * (b + 1)]
            for g in range(1, groups):
                block = block + both[probe_count * g : probe_count * (g + 1), LANES * (b + g) : LANES * (b + g + 1)]
            part[probe_count * b : probe_count * (b + 1), :] = block.astype(BF)

    part_copies = []
    for off in range(1, n_tr):
        dst = lax.rem(tr + off, n_tr)
        c = copy(
            part.at[pl.ds(pl.multiple_of(dst * share, share), share), :], parts_in.at[tr],
            part_send.at[off], part_recv.at[off], trace=dst,
        )
        c.start()
        pending.append(c)
    summed = part[pl.ds(pl.multiple_of(tr * share, share), share), :].astype(F32)
    for off in range(1, n_tr):
        src = lax.rem(tr + n_tr - off, n_tr)
        copy(
            part.at[pl.ds(0, share), :], parts_in.at[src], part_send.at[off], part_recv.at[off], trace=src
        ).wait_recv()
        summed = summed + parts_in[src].astype(F32)
    sketch[tm, pl.ds(pl.multiple_of(tr * share, share), share), :] = summed.astype(BF)

    def place(zo, ro, parity):
        t = lax.rem(z + n_z - zo, n_z) * 2 + parity
        r = lax.rem(tr + n_tr - ro, n_tr)
        return sketch.at[t, pl.ds(pl.multiple_of(r * share, share), share), :]

    def along_z(zo):
        here = place(0, 0, core)
        return copy(here, here, z_send.at[zo], z_recv.at[zo], tm=lax.rem(z + zo, n_z) * 2 + core)

    def across(zo, ro):
        here = place(zo, 0, core)
        return copy(here, here, x_send.at[zo, ro], x_recv.at[zo, ro], trace=lax.rem(tr + ro, n_tr))

    def to_sibling(zo, ro):
        here = place(zo, ro, core)
        return copy(here, here, c_send.at[zo, ro], c_recv.at[zo, ro], tm=z * 2 + 1 - core)

    def go(c):
        c.start()
        pending.append(c)

    def arrived(zo, ro, send, recv, parity):
        there = place(zo, ro, parity)
        copy(there, there, send, recv, tm=z * 2 + 1 - core).wait_recv()

    for zo in range(1, n_z):
        go(along_z(zo))
    for ro in range(1, n_tr):
        go(across(0, ro))
    go(to_sibling(0, 0))

    for off in range(1, n_tm):
        src = lax.rem(tm + n_tm - off, n_tm)
        copy(slices.at[src], windows.at[src], win_send.at[off], win_recv.at[off], tm=src).wait_recv()
    rows = lax.broadcasted_iota(jnp.int32, (LANES, LANES), 0)
    lanes = lax.broadcasted_iota(jnp.int32, (LANES, LANES), 1)

    @jax.named_scope("hankel")
    def hankel_of(c):
        ahead = jnp.zeros((LANES, LANES), F32)
        for m in range(total + groups - 2, -1, -1):
            if m < total:
                t, b = m // chunks, m % chunks
                line = windows[t, c : c + 1, LANES * b : LANES * (b + 1)]
                now = pltpu.roll(jnp.broadcast_to(line, (LANES, LANES)), 1, 1, stride=1, stride_axis=0)
            else:
                now = jnp.zeros((LANES, LANES), F32)
            hankel[LANES * c : LANES * (c + 1), LANES * m : LANES * (m + 1)] = jnp.where(
                lanes <= rows, now, ahead
            ).astype(BF)
            ahead = now

    @jax.named_scope("gram")
    def gram_of(t):
        for b in range(chunks):
            flat[t, :, LANES * b : LANES * (b + 1)] = sketch[t, probe_count * b : probe_count * (b + 1), :]
        return nt(flat[t], flat[t])

    for c in range(own // 2):
        hankel_of(c)
    for zo in range(1, n_z):
        arrived(zo, 0, z_send.at[zo], z_recv.at[zo], core)
        for ro in range(1, n_tr):
            go(across(zo, ro))
        go(to_sibling(zo, 0))
    for c in range(own // 2, own):
        hankel_of(c)
    gram = jnp.zeros((probe_count, probe_count), F32)
    for zo in range(n_z):
        for ro in range(1, n_tr):
            arrived(zo, ro, x_send.at[zo, ro], x_recv.at[zo, ro], core)
            go(to_sibling(zo, ro))
        gram = gram + gram_of(lax.rem(z + n_z - zo, n_z) * 2 + core)
    for zo in range(n_z):
        for ro in range(n_tr):
            arrived(zo, ro, c_send.at[zo, ro], c_recv.at[zo, ro], 1 - core)
        gram = gram + gram_of(lax.rem(z + n_z - zo, n_z) * 2 + 1 - core)

    with jax.named_scope("inverse_factor"):
        splits = jnp.concatenate(split3(inverse_factor(gram)), axis=0)
    with jax.named_scope("basis"):
        for g in range(groups):
            rows_g = slice(probe_count * g, probe_count * (g + 1))
            if g:
                spread[rows_g, : LANES * g] = jnp.zeros((probe_count, LANES * g), BF)
            if g < groups - 1:
                spread[rows_g, LANES * (total + g) :] = jnp.zeros((probe_count, LANES * (groups - 1 - g)), BF)
        for t in range(n_tm):
            product = nn(splits, flat[t])
            hi, mid, low = (product[probe_count * i : probe_count * (i + 1)] for i in range(3))
            basis = (low + mid + hi).astype(BF)
            for g in range(groups):
                spread[probe_count * g : probe_count * (g + 1), width * t + LANES * g : width * (t + 1) + LANES * g] = basis
    with jax.named_scope("coefs"):
        coefs = nt(hankel[...], spread[...]).astype(BF)
        flip = jnp.where(lanes + rows == LANES - 1, 1.0, 0.0).astype(BF)
        coefs = jnp.concatenate(
            [nn(flip, coefs[LANES * c : LANES * (c + 1)]).astype(BF) for c in range(own)], axis=0
        )
    with jax.named_scope("antidiagonals"):
        carry = [jnp.zeros((SUB, LANES), F32) for _ in range(own)]
        for t in range(n_tm):
            product = nn(coefs, spread[:, width * t : width * (t + 1)])
            for c in range(own):
                for b in range(chunks):
                    block = product[LANES * c : LANES * (c + 1), LANES * b : LANES * (b + 1)]
                    turned = pltpu.roll(block, 0, 1, stride=1, stride_axis=0)
                    inside = jnp.where(lanes >= rows, turned, 0.0)
                    beyond = turned - inside
                    near = carry[c]
                    far = jnp.zeros((SUB, LANES), F32)
                    for a in range(LANES // SUB):
                        near = near + inside[SUB * a : SUB * (a + 1)]
                        far = far + beyond[SUB * a : SUB * (a + 1)]
                    carry[c] = far
                    est_out[t, c : c + 1, LANES * b : LANES * (b + 1)] = jnp.sum(near, axis=0, keepdims=True)

    for off in range(1, n_tm):
        dst = lax.rem(tm + off, n_tm)
        go(copy(est_out.at[dst], est_in.at[tm], est_send.at[off], est_recv.at[off], tm=dst))
    est_in[tm] = est_out[tm]
    for off in range(1, n_tm):
        src = lax.rem(tm + n_tm - off, n_tm)
        copy(est_out.at[src], est_in.at[src], est_send.at[off], est_recv.at[off], tm=src).wait_recv()
    for i in range(n_tm):
        out[own * i : own * (i + 1), :] = est_in[i]
    for c in pending:
        c.wait_send()


def on_device(observed, sampled, probes):
    n_tm, n_tr = lax.axis_size("tm"), lax.axis_size("trace")
    taps, traces, count = probes.shape
    width = observed.shape[1]
    groups = taps // LANES
    chunks = width // LANES
    total = n_tm * chunks
    own = traces // n_tm
    n_z = n_tm // 2
    probes = probes.reshape(groups, LANES * traces, count)
    vmem = pl.BlockSpec(memory_space=pltpu.VMEM)
    dma = pltpu.SemaphoreType.DMA
    summed = pl.pallas_call(
        functools.partial(kernel, n_tm, n_tr),
        out_shape=jax.ShapeDtypeStruct((traces, width), F32),
        in_specs=[vmem, vmem, pl.BlockSpec(memory_space=pl.ANY)],
        out_specs=vmem,
        scratch_shapes=[
            pltpu.VMEM(probes.shape, BF), dma,
            pltpu.VMEM((traces, width), BF),
            pltpu.VMEM((traces, taps), BF),
            pltpu.VMEM((n_tm, own, width), F32),
            pltpu.VMEM((n_tm, own, width), F32),
            pltpu.VMEM((LANES * traces, width + taps - LANES), BF),
            pltpu.VMEM((groups * count, LANES * traces), BF),
            pltpu.VMEM((chunks * count, LANES), BF),
            pltpu.VMEM((n_tr, chunks * count // n_tr, LANES), BF),
            pltpu.VMEM((n_tm, chunks * count, LANES), BF),
            pltpu.VMEM((n_tm, count, width), BF),
            pltpu.VMEM((own * LANES, (total + groups - 1) * LANES), BF),
            pltpu.VMEM((groups * count, (total + groups - 1) * LANES), BF),
            pltpu.VMEM((n_tm, own, width), F32),
            pltpu.VMEM((n_tm, own, width), F32),
            dma((2,)),
            dma((n_tm,)), dma((n_tm,)),
            dma((n_tr,)), dma((n_tr,)),
            dma((n_z,)), dma((n_z,)),
            dma((n_z, n_tr)), dma((n_z, n_tr)),
            dma((n_z, n_tr)), dma((n_z, n_tr)),
            dma((n_tm,)), dma((n_tm,)),
        ],
        compiler_params=pltpu.CompilerParams(
            collective_id=0, has_side_effects=True, vmem_limit_bytes=56 * 1024 * 1024
        ),
        cost_estimate=pl.CostEstimate(flops=2 * 10**9, bytes_accessed=2 * 10**6, transcendentals=0),
    )(observed, sampled, probes)
    position = lax.axis_index("tm") * width + jnp.arange(width, dtype=jnp.int32)
    counts = jnp.minimum(position + 1, taps).astype(F32)
    return jnp.where(sampled == 1, observed.astype(F32), summed / counts[None, :])


def solution(mesh):
    in_specs = (P("trace", "tm"), P("trace", "tm"), P(None, "trace", None))
    out_specs = P("trace", "tm")
    return jax.shard_map(
        on_device, mesh=mesh, in_specs=in_specs, out_specs=out_specs, check_vma=False
    )
```

```python
import functools

import jax
import jax.numpy as jnp
from jax import lax
from jax.experimental import pallas as pl
from jax.experimental.pallas import tpu as pltpu
from jax.sharding import PartitionSpec as P

LANES = 128
SUB = 8
BF = jnp.bfloat16
F32 = jnp.float32


def nt(a, b):
    return lax.dot_general(a, b, (((1,), (1,)), ((), ())), preferred_element_type=F32)


def nn(a, b):
    return lax.dot_general(a, b, (((1,), (0,)), ((), ())), preferred_element_type=F32)


def split3(x):
    hi = x.astype(BF)
    rest = x - hi.astype(F32)
    mid = rest.astype(BF)
    low = (rest - mid.astype(F32)).astype(BF)
    return hi, mid, low


def panel_step(step, size, below, left, right, found):
    rows = lax.broadcasted_iota(jnp.int32, (SUB, size), 0)

    def at(x, s):
        return jnp.broadcast_to(x[s : s + 1], (SUB, size))

    panel = [left[0:SUB, :], right[0:SUB, :]]
    wide = [jnp.broadcast_to(panel[0][:, q : q + 1], (SUB, size)) for q in range(SUB)]
    taken = jnp.zeros((SUB, size), F32)
    scale = jnp.ones((SUB, size), F32)
    for s in range(0, SUB, 2):
        first, second = wide[s], wide[s + 1]
        p, q, r = at(first, s), at(first, s + 1), at(second, s + 1)
        det = p * r - q * q
        inverse = 1.0 / det
        here = (rows == s) | (rows == s + 1)
        f0, f1 = jnp.where(here, 0.0, first), jnp.where(here, 0.0, second)

        def eliminate(x):
            x0, x1 = at(x, s), at(x, s + 1)
            y0 = (r * x0 - q * x1) * inverse
            y1 = (p * x1 - q * x0) * inverse
            rest = jnp.where(rows == s, y0, jnp.where(rows == s + 1, y1, x))
            return rest - (f0 * y0 + f1 * y1)

        x0, x1 = at(panel[1], s), at(panel[1], s + 1)
        taken = jnp.where(rows == s, x0, jnp.where(rows == s + 1, x1 - (q / p) * x0, taken))
        scale = jnp.where(rows == s, p, jnp.where(rows == s + 1, det / p, scale))
        for k in range(s + 2, SUB):
            wide[k] = eliminate(wide[k])
        panel = [eliminate(x) for x in panel]
    found[pl.ds(pl.multiple_of(step * SUB, SUB), SUB), :] = taken * lax.rsqrt(scale)
    solved = [[at(x, s) for s in range(SUB)] for x in panel]
    for a in range(1, below + 1):
        here, up = slice(SUB * a, SUB * (a + 1)), slice(SUB * (a - 1), SUB * a)
        x, y = left[here, :], right[here, :]
        factors = [jnp.broadcast_to(x[:, q : q + 1], (SUB, size)) for q in range(SUB)]
        for q in range(SUB):
            x = x - factors[q] * solved[0][q]
            y = y - factors[q] * solved[1][q]
        left[up, :] = pltpu.roll(x, size - SUB, 1)
        right[up, :] = y


def inverse_factor(gram, left, right, found):
    size = gram.shape[0]
    rows = lax.broadcasted_iota(jnp.int32, (size, size), 0)
    lanes = lax.broadcasted_iota(jnp.int32, (size, size), 1)
    diagonal = jnp.where(rows == lanes, gram, 0.0)
    by_row = lax.rsqrt(jnp.sum(diagonal, axis=1, keepdims=True))
    by_lane = lax.rsqrt(jnp.sum(diagonal, axis=0, keepdims=True))
    left[...] = gram * by_row * by_lane
    right[...] = jnp.where(rows == lanes, 1.0, 0.0).astype(F32)
    blocks = size // SUB
    half = blocks // 2

    @pl.loop(0, half)
    def _(step):
        panel_step(step, size, blocks - 1, left, right, found)

    @pl.loop(half, blocks)
    def _(step):
        panel_step(step, size, blocks - half - 1, left, right, found)

    return found[...] * by_lane


def kernel(
    n_tm, n_tr,
    observed, sampled, probes_in, out,
    probes, probes_sem, data, halo, slices, windows, rolled, probes_t, part, parts_in, sketch, flat,
    hankel, spread, est_out, est_in, left, right, found, total_coefs,
    halo_sems, win_send, win_recv, part_send, part_recv,
    z_send, z_recv, x_send, x_recv, c_send, c_recv, est_send, est_recv,
):
    tm = lax.axis_index("tm")
    tr = lax.axis_index("trace")
    n_z = n_tm // 2
    z = tm // 2
    core = lax.rem(tm, 2)
    traces, width = data.shape
    own = traces // n_tm
    groups, contract, probe_count = probes.shape
    fetch = pltpu.make_async_copy(probes_in, probes, probes_sem)
    fetch.start()
    taps = groups * LANES
    chunks = width // LANES
    total = n_tm * chunks
    samples = n_tm * width
    share = part.shape[0] // n_tr

    def copy(src, dst, send, recv, **to):
        return pltpu.make_async_remote_copy(
            src_ref=src, dst_ref=dst, send_sem=send, recv_sem=recv,
            device_id=to, device_id_type=pl.DeviceIdType.MESH,
        )

    barrier = pltpu.get_barrier_semaphore()
    for off in range(1, n_tm):
        pl.semaphore_signal(barrier, inc=1, device_id={"tm": lax.rem(tm + off, n_tm)}, device_id_type=pl.DeviceIdType.MESH)
    for off in range(1, n_tr):
        pl.semaphore_signal(barrier, inc=1, device_id={"trace": lax.rem(tr + off, n_tr)}, device_id_type=pl.DeviceIdType.MESH)

    masked = jnp.where(sampled[...] == 1, observed[...].astype(F32), 0.0)
    data[...] = masked.astype(BF)
    for i in range(n_tm):
        slices[i] = masked[own * i : own * (i + 1)]
    pl.semaphore_wait(barrier, n_tm + n_tr - 2)

    pending = []
    before = lax.rem(tm + n_tm - 1, n_tm)
    halo_copy = copy(data.at[:, pl.ds(0, taps)], halo, halo_sems.at[0], halo_sems.at[1], tm=before)
    halo_copy.start()
    pending.append(halo_copy)
    for off in range(1, n_tm):
        dst = lax.rem(tm + off, n_tm)
        c = copy(slices.at[dst], windows.at[tm], win_send.at[off], win_recv.at[off], tm=dst)
        c.start()
        pending.append(c)
    windows[tm] = slices[tm]

    fetch.wait()
    with jax.named_scope("probes_transposed"):
        @pl.loop(0, contract // LANES, unroll=2)
        def _(i):
            some = pl.ds(pl.multiple_of(i * LANES, LANES), LANES)
            for g in range(groups):
                probes_t[probe_count * g : probe_count * (g + 1), some] = probes[g, some, :].T

    halo_copy.wait_recv()
    with jax.named_scope("sketch_part"):
        tail = jnp.where(tm < n_tm - 1, halo[...].astype(F32), 0.0)
        extended = jnp.concatenate([masked, tail], axis=1)
        keep = rolled.shape[1]
        lane = lax.broadcasted_iota(jnp.int32, (traces, LANES), 1)
        parts = [extended[:, LANES * m : LANES * (m + 1)] for m in range(keep // LANES + 1)]

        @pl.loop(0, LANES, unroll=8)
        def _(j):
            turned = [pltpu.roll(x, lax.rem(LANES - j, LANES), 1) for x in parts]
            moved = [jnp.where(lane < LANES - j, x, y).astype(BF) for x, y in zip(turned, turned[1:])]
            rolled[pl.ds(pl.multiple_of(j * traces, traces), traces), :] = jnp.concatenate(moved, axis=1)

        both = nn(probes_t[...], rolled[...])
        for b in range(chunks):
            block = both[:probe_count, LANES * b : LANES * (b + 1)]
            for g in range(1, groups):
                block = block + both[probe_count * g : probe_count * (g + 1), LANES * (b + g) : LANES * (b + g + 1)]
            part[probe_count * b : probe_count * (b + 1), :] = block.astype(BF)

    part_copies = []
    for off in range(1, n_tr):
        dst = lax.rem(tr + off, n_tr)
        c = copy(
            part.at[pl.ds(pl.multiple_of(dst * share, share), share), :], parts_in.at[tr],
            part_send.at[off], part_recv.at[off], trace=dst,
        )
        c.start()
        pending.append(c)
    summed = part[pl.ds(pl.multiple_of(tr * share, share), share), :].astype(F32)
    for off in range(1, n_tr):
        src = lax.rem(tr + n_tr - off, n_tr)
        copy(
            part.at[pl.ds(0, share), :], parts_in.at[src], part_send.at[off], part_recv.at[off], trace=src
        ).wait_recv()
        summed = summed + parts_in[src].astype(F32)
    sketch[tm, pl.ds(pl.multiple_of(tr * share, share), share), :] = summed.astype(BF)

    def place(zo, ro, parity):
        t = lax.rem(z + n_z - zo, n_z) * 2 + parity
        r = lax.rem(tr + n_tr - ro, n_tr)
        return sketch.at[t, pl.ds(pl.multiple_of(r * share, share), share), :]

    def along_z(zo):
        here = place(0, 0, core)
        return copy(here, here, z_send.at[zo], z_recv.at[zo], tm=lax.rem(z + zo, n_z) * 2 + core)

    def across(zo, ro):
        here = place(zo, 0, core)
        return copy(here, here, x_send.at[zo, ro], x_recv.at[zo, ro], trace=lax.rem(tr + ro, n_tr))

    def to_sibling(zo, ro):
        here = place(zo, ro, core)
        return copy(here, here, c_send.at[zo, ro], c_recv.at[zo, ro], tm=z * 2 + 1 - core)

    def go(c):
        c.start()
        pending.append(c)

    def arrived(zo, ro, send, recv, parity):
        there = place(zo, ro, parity)
        copy(there, there, send, recv, tm=z * 2 + 1 - core).wait_recv()

    for zo in range(1, n_z):
        go(along_z(zo))
    for ro in range(1, n_tr):
        go(across(0, ro))
    go(to_sibling(0, 0))

    for off in range(1, n_tm):
        src = lax.rem(tm + n_tm - off, n_tm)
        copy(slices.at[src], windows.at[src], win_send.at[off], win_recv.at[off], tm=src).wait_recv()
    rows = lax.broadcasted_iota(jnp.int32, (LANES, LANES), 0)
    lanes = lax.broadcasted_iota(jnp.int32, (LANES, LANES), 1)

    for k in range(groups - 1):
        hankel[:, LANES * (total + k) :] = jnp.zeros((own * LANES, LANES * (groups - 1 - k)), BF)

    @jax.named_scope("hankel")
    def hankel_of(c):
        def turned(t, b):
            line = windows[t, c : c + 1, LANES * b : LANES * (b + 1)]
            return pltpu.roll(jnp.broadcast_to(line, (LANES, LANES)), 1, 1, stride=1, stride_axis=0)

        def some(i, ahead):
            t = n_tm - 1 - i
            for b in range(chunks - 1, -1, -1):
                now = turned(t, b)
                to = pl.ds(pl.multiple_of(t * width + LANES * b, LANES), LANES)
                hankel[LANES * c : LANES * (c + 1), to] = jnp.where(lanes <= rows, now, ahead).astype(BF)
                ahead = now
            return ahead

        lax.fori_loop(0, n_tm, some, jnp.zeros((LANES, LANES), F32))

    @jax.named_scope("gram")
    def gram_of(t):
        for b in range(chunks):
            flat[t, :, LANES * b : LANES * (b + 1)] = sketch[t, probe_count * b : probe_count * (b + 1), :]
        return nt(flat[t], flat[t])

    for c in range(own // 2):
        hankel_of(c)
    for zo in range(1, n_z):
        arrived(zo, 0, z_send.at[zo], z_recv.at[zo], core)
        for ro in range(1, n_tr):
            go(across(zo, ro))
        go(to_sibling(zo, 0))
    for c in range(own // 2, own):
        hankel_of(c)
    def from_across(zo, gram):
        for ro in range(1, n_tr):
            arrived(zo, ro, x_send.at[zo, ro], x_recv.at[zo, ro], core)
            to_sibling(zo, ro).start()
        return gram + gram_of(lax.rem(z + n_z - zo, n_z) * 2 + core)

    def from_sibling(zo, gram):
        for ro in range(n_tr):
            arrived(zo, ro, c_send.at[zo, ro], c_recv.at[zo, ro], 1 - core)
        return gram + gram_of(lax.rem(z + n_z - zo, n_z) * 2 + 1 - core)

    gram = lax.fori_loop(0, n_z, from_across, jnp.zeros((probe_count, probe_count), F32))
    gram = lax.fori_loop(0, n_z, from_sibling, gram)

    with jax.named_scope("inverse_factor"):
        splits = jnp.concatenate(split3(inverse_factor(gram, left, right, found)), axis=0)
    with jax.named_scope("basis"):
        for g in range(groups):
            rows_g = slice(probe_count * g, probe_count * (g + 1))
            if g:
                spread[rows_g, : LANES * g] = jnp.zeros((probe_count, LANES * g), BF)
            if g < groups - 1:
                spread[rows_g, LANES * (total + g) :] = jnp.zeros((probe_count, LANES * (groups - 1 - g)), BF)

        @pl.loop(0, n_tm)
        def _(t):
            product = nn(splits, flat[t])
            hi, mid, low = (product[probe_count * i : probe_count * (i + 1)] for i in range(3))
            basis = (low + mid + hi).astype(BF)
            for g in range(groups):
                to = pl.ds(pl.multiple_of(t * width + LANES * g, LANES), width)
                spread[probe_count * g : probe_count * (g + 1), to] = basis
    with jax.named_scope("coefs"):
        total_coefs[...] = nt(hankel[:, LANES * total :], spread[:, LANES * total :])

        @pl.loop(0, n_tm // 2)
        def _(i):
            some = pl.ds(pl.multiple_of(i * 2 * width, LANES), 2 * width)
            total_coefs[...] += nt(hankel[:, some], spread[:, some])

        coefs = total_coefs[...].astype(BF)
        flip = jnp.where(lanes + rows == LANES - 1, 1.0, 0.0).astype(BF)
        coefs = jnp.concatenate(
            [nn(flip, coefs[LANES * c : LANES * (c + 1)]).astype(BF) for c in range(own)], axis=0
        )
    with jax.named_scope("antidiagonals"):
        def some_sums(t, carry):
            carry = list(carry)
            product = nn(coefs, spread[:, pl.ds(pl.multiple_of(t * width, LANES), width)])
            for c in range(own):
                for b in range(chunks):
                    block = product[LANES * c : LANES * (c + 1), LANES * b : LANES * (b + 1)]
                    turned = pltpu.roll(block, 0, 1, stride=1, stride_axis=0)
                    inside = jnp.where(lanes >= rows, turned, 0.0)
                    beyond = turned - inside
                    near = carry[c]
                    far = jnp.zeros((SUB, LANES), F32)
                    for a in range(LANES // SUB):
                        near = near + inside[SUB * a : SUB * (a + 1)]
                        far = far + beyond[SUB * a : SUB * (a + 1)]
                    carry[c] = far
                    est_out[t, c : c + 1, LANES * b : LANES * (b + 1)] = jnp.sum(near, axis=0, keepdims=True)
            return tuple(carry)

        lax.fori_loop(0, n_tm, some_sums, tuple(jnp.zeros((SUB, LANES), F32) for _ in range(own)))

    for off in range(1, n_tm):
        dst = lax.rem(tm + off, n_tm)
        go(copy(est_out.at[dst], est_in.at[tm], est_send.at[off], est_recv.at[off], tm=dst))
    est_in[tm] = est_out[tm]
    for off in range(1, n_tm):
        src = lax.rem(tm + n_tm - off, n_tm)
        copy(est_out.at[src], est_in.at[src], est_send.at[off], est_recv.at[off], tm=src).wait_recv()
    for i in range(n_tm):
        out[own * i : own * (i + 1), :] = est_in[i]
    @pl.loop(0, n_z)
    def _(zo):
        for ro in range(1, n_tr):
            to_sibling(zo, ro).wait_send()

    for c in pending:
        c.wait_send()


def on_device(observed, sampled, probes):
    n_tm, n_tr = lax.axis_size("tm"), lax.axis_size("trace")
    taps, traces, count = probes.shape
    width = observed.shape[1]
    groups = taps // LANES
    chunks = width // LANES
    total = n_tm * chunks
    own = traces // n_tm
    n_z = n_tm // 2
    probes = probes.reshape(groups, LANES * traces, count)
    vmem = pl.BlockSpec(memory_space=pltpu.VMEM)
    dma = pltpu.SemaphoreType.DMA
    summed = pl.pallas_call(
        functools.partial(kernel, n_tm, n_tr),
        out_shape=jax.ShapeDtypeStruct((traces, width), F32),
        in_specs=[vmem, vmem, pl.BlockSpec(memory_space=pl.ANY)],
        out_specs=vmem,
        scratch_shapes=[
            pltpu.VMEM(probes.shape, BF), dma,
            pltpu.VMEM((traces, width), BF),
            pltpu.VMEM((traces, taps), BF),
            pltpu.VMEM((n_tm, own, width), F32),
            pltpu.VMEM((n_tm, own, width), F32),
            pltpu.VMEM((LANES * traces, width + taps - LANES), BF),
            pltpu.VMEM((groups * count, LANES * traces), BF),
            pltpu.VMEM((chunks * count, LANES), BF),
            pltpu.VMEM((n_tr, chunks * count // n_tr, LANES), BF),
            pltpu.VMEM((n_tm, chunks * count, LANES), BF),
            pltpu.VMEM((n_tm, count, width), BF),
            pltpu.VMEM((own * LANES, (total + groups - 1) * LANES), BF),
            pltpu.VMEM((groups * count, (total + groups - 1) * LANES), BF),
            pltpu.VMEM((n_tm, own, width), F32),
            pltpu.VMEM((n_tm, own, width), F32),
            pltpu.VMEM((count, count), F32),
            pltpu.VMEM((count, count), F32),
            pltpu.VMEM((count, count), F32),
            pltpu.VMEM((own * LANES, groups * count), F32),
            dma((2,)),
            dma((n_tm,)), dma((n_tm,)),
            dma((n_tr,)), dma((n_tr,)),
            dma((n_z,)), dma((n_z,)),
            dma((n_z, n_tr)), dma((n_z, n_tr)),
            dma((n_z, n_tr)), dma((n_z, n_tr)),
            dma((n_tm,)), dma((n_tm,)),
        ],
        compiler_params=pltpu.CompilerParams(
            collective_id=0, has_side_effects=True, vmem_limit_bytes=56 * 1024 * 1024
        ),
        cost_estimate=pl.CostEstimate(flops=2 * 10**9, bytes_accessed=2 * 10**6, transcendentals=0),
    )(observed, sampled, probes)
    position = lax.axis_index("tm") * width + jnp.arange(width, dtype=jnp.int32)
    counts = jnp.minimum(position + 1, taps).astype(F32)
    return jnp.where(sampled == 1, observed.astype(F32), summed / counts[None, :])


def solution(mesh):
    in_specs = (P("trace", "tm"), P("trace", "tm"), P(None, "trace", None))
    out_specs = P("trace", "tm")
    return jax.shard_map(
        on_device, mesh=mesh, in_specs=in_specs, out_specs=out_specs, check_vma=False
    )
```

```python
import functools

import jax
import jax.numpy as jnp
from jax import lax
from jax.experimental import pallas as pl
from jax.experimental.pallas import tpu as pltpu
from jax.sharding import PartitionSpec as P

LANES = 128
SUB = 8
BF = jnp.bfloat16
F32 = jnp.float32


def nt(a, b, precision=None):
    return lax.dot_general(a, b, (((1,), (1,)), ((), ())), precision=precision, preferred_element_type=F32)


def nn(a, b):
    return lax.dot_general(a, b, (((1,), (0,)), ((), ())), preferred_element_type=F32)


def split3(x):
    hi = x.astype(BF)
    rest = x - hi.astype(F32)
    mid = rest.astype(BF)
    low = (rest - mid.astype(F32)).astype(BF)
    return hi, mid, low


def inverse_factor(gram):
    size = gram.shape[0]
    blocks = size // SUB
    full_rows = lax.broadcasted_iota(jnp.int32, (size, size), 0)
    full_lanes = lax.broadcasted_iota(jnp.int32, (size, size), 1)
    diagonal = jnp.where(full_rows == full_lanes, gram, 0.0)
    by_row = lax.rsqrt(jnp.sum(diagonal, axis=1, keepdims=True))
    by_lane = lax.rsqrt(jnp.sum(diagonal, axis=0, keepdims=True))
    gram = gram * by_row * by_lane
    rows = lax.broadcasted_iota(jnp.int32, (SUB, size), 0)
    lanes = lax.broadcasted_iota(jnp.int32, (SUB, size), 1)
    left = [gram[SUB * a : SUB * (a + 1)] for a in range(blocks)]
    right = [jnp.where(lanes == rows + SUB * a, 1.0, 0.0).astype(F32) for a in range(blocks)]
    found = []

    def at(x, s):
        return jnp.broadcast_to(x[s : s + 1], (SUB, size))

    for a0 in range(blocks):
        columns = {
            a: [jnp.broadcast_to(left[a][:, SUB * a0 + q : SUB * a0 + q + 1], (SUB, size)) for q in range(SUB)]
            for a in range(a0, blocks)
        }
        wide = columns.pop(a0)
        panel = {"left": left[a0], "right": right[a0]}
        taken = jnp.zeros((SUB, size), F32)
        scale = jnp.ones((SUB, size), F32)
        for s in range(0, SUB, 2):
            first, second = wide[s], wide[s + 1]
            p, q, r = at(first, s), at(first, s + 1), at(second, s + 1)
            det = p * r - q * q
            inverse = 1.0 / det
            here = (rows == s) | (rows == s + 1)
            f0, f1 = jnp.where(here, 0.0, first), jnp.where(here, 0.0, second)

            def eliminate(x):
                x0, x1 = at(x, s), at(x, s + 1)
                y0 = (r * x0 - q * x1) * inverse
                y1 = (p * x1 - q * x0) * inverse
                rest = jnp.where(rows == s, y0, jnp.where(rows == s + 1, y1, x))
                return rest - (f0 * y0 + f1 * y1)

            x0, x1 = at(panel["right"], s), at(panel["right"], s + 1)
            taken = jnp.where(rows == s, x0, jnp.where(rows == s + 1, x1 - (q / p) * x0, taken))
            scale = jnp.where(rows == s, p, jnp.where(rows == s + 1, det / p, scale))
            for k in range(s + 2, SUB):
                wide[k] = eliminate(wide[k])
            panel = {side: eliminate(x) for side, x in panel.items()}
        found.append(taken * lax.rsqrt(scale))
        solved_left = [at(panel["left"], s) for s in range(SUB)]
        solved_right = [at(panel["right"], s) for s in range(SUB)]
        for a in range(a0 + 1, blocks):
            for q in range(SUB):
                left[a] = left[a] - columns[a][q] * solved_left[q]
                right[a] = right[a] - columns[a][q] * solved_right[q]
    return jnp.concatenate(found, axis=0) * by_lane


def kernel(
    n_tm, n_tr,
    observed, sampled, probes_in, out,
    probes, probes_sem, data, halo, slices, windows, rolled, probes_t, part, parts_in, sketch, flat,
    hankel, spread, projected, est_out, est_in,
    halo_sems, win_send, win_recv, part_send, part_recv,
    z_send, z_recv, x_send, x_recv, c_send, c_recv, est_send, est_recv,
):
    tm = lax.axis_index("tm")
    tr = lax.axis_index("trace")
    n_z = n_tm // 2
    z = tm // 2
    core = lax.rem(tm, 2)
    traces, width = data.shape
    own = traces // n_tm
    groups, contract, probe_count = probes.shape
    fetch = pltpu.make_async_copy(probes_in, probes, probes_sem)
    fetch.start()
    taps = groups * LANES
    chunks = width // LANES
    total = n_tm * chunks
    samples = n_tm * width
    share = part.shape[0] // n_tr

    def copy(src, dst, send, recv, **to):
        return pltpu.make_async_remote_copy(
            src_ref=src, dst_ref=dst, send_sem=send, recv_sem=recv,
            device_id=to, device_id_type=pl.DeviceIdType.MESH,
        )

    barrier = pltpu.get_barrier_semaphore()
    for off in range(1, n_tm):
        pl.semaphore_signal(barrier, inc=1, device_id={"tm": lax.rem(tm + off, n_tm)}, device_id_type=pl.DeviceIdType.MESH)
    for off in range(1, n_tr):
        pl.semaphore_signal(barrier, inc=1, device_id={"trace": lax.rem(tr + off, n_tr)}, device_id_type=pl.DeviceIdType.MESH)

    masked = jnp.where(sampled[...] == 1, observed[...].astype(F32), 0.0)
    data[...] = masked.astype(BF)
    for i in range(n_tm):
        slices[i] = masked[own * i : own * (i + 1)]
    pl.semaphore_wait(barrier, n_tm + n_tr - 2)

    pending = []
    before = lax.rem(tm + n_tm - 1, n_tm)
    halo_copy = copy(data.at[:, pl.ds(0, taps)], halo, halo_sems.at[0], halo_sems.at[1], tm=before)
    halo_copy.start()
    pending.append(halo_copy)
    for off in range(1, n_tm):
        dst = lax.rem(tm + off, n_tm)
        c = copy(slices.at[dst], windows.at[tm], win_send.at[off], win_recv.at[off], tm=dst)
        c.start()
        pending.append(c)
    windows[tm] = slices[tm]

    fetch.wait()
    with jax.named_scope("probes_transposed"):
        for g in range(groups):
            probes_t[probe_count * g : probe_count * (g + 1), :] = probes[g].T

    halo_copy.wait_recv()
    with jax.named_scope("sketch_part"):
        tail = jnp.where(tm < n_tm - 1, halo[...].astype(F32), 0.0)
        extended = jnp.concatenate([masked, tail], axis=1)
        reach = extended.shape[1]
        keep = rolled.shape[1]
        both = jnp.zeros((groups * probe_count, keep), F32)
        step = LANES // 4
        for first in range(0, LANES, step):
            for j in range(first, first + step):
                moved = pltpu.roll(extended, reach - j, 1) if j else extended
                rolled[traces * j : traces * (j + 1), :] = moved[:, :keep].astype(BF)
            some = slice(traces * first, traces * (first + step))
            both = both + nn(probes_t[:, some], rolled[some, :])
        for b in range(chunks):
            block = both[:probe_count, LANES * b : LANES * (b + 1)]
            for g in range(1, groups):
                block = block + both[probe_count * g : probe_count * (g + 1), LANES * (b + g) : LANES * (b + g + 1)]
            part[probe_count * b : probe_count * (b + 1), :] = block.astype(BF)

    part_copies = []
    for off in range(1, n_tr):
        dst = lax.rem(tr + off, n_tr)
        c = copy(
            part.at[pl.ds(pl.multiple_of(dst * share, share), share), :], parts_in.at[tr],
            part_send.at[off], part_recv.at[off], trace=dst,
        )
        c.start()
        pending.append(c)
    summed = part[pl.ds(pl.multiple_of(tr * share, share), share), :].astype(F32)
    for off in range(1, n_tr):
        src = lax.rem(tr + n_tr - off, n_tr)
        copy(
            part.at[pl.ds(0, share), :], parts_in.at[src], part_send.at[off], part_recv.at[off], trace=src
        ).wait_recv()
        summed = summed + parts_in[src].astype(F32)
    sketch[tm, pl.ds(pl.multiple_of(tr * share, share), share), :] = summed.astype(BF)

    def place(zo, ro, parity):
        t = lax.rem(z + n_z - zo, n_z) * 2 + parity
        r = lax.rem(tr + n_tr - ro, n_tr)
        return sketch.at[t, pl.ds(pl.multiple_of(r * share, share), share), :]

    def along_z(zo):
        here = place(0, 0, core)
        return copy(here, here, z_send.at[zo], z_recv.at[zo], tm=lax.rem(z + zo, n_z) * 2 + core)

    def across(zo, ro):
        here = place(zo, 0, core)
        return copy(here, here, x_send.at[zo, ro], x_recv.at[zo, ro], trace=lax.rem(tr + ro, n_tr))

    def to_sibling(zo, ro):
        here = place(zo, ro, core)
        return copy(here, here, c_send.at[zo, ro], c_recv.at[zo, ro], tm=z * 2 + 1 - core)

    def go(c):
        c.start()
        pending.append(c)

    def arrived(zo, ro, send, recv, parity):
        there = place(zo, ro, parity)
        copy(there, there, send, recv, tm=z * 2 + 1 - core).wait_recv()

    for zo in range(1, n_z):
        go(along_z(zo))
    for ro in range(1, n_tr):
        go(across(0, ro))
    go(to_sibling(0, 0))

    for off in range(1, n_tm):
        src = lax.rem(tm + n_tm - off, n_tm)
        copy(slices.at[src], windows.at[src], win_send.at[off], win_recv.at[off], tm=src).wait_recv()
    rows = lax.broadcasted_iota(jnp.int32, (LANES, LANES), 0)
    lanes = lax.broadcasted_iota(jnp.int32, (LANES, LANES), 1)

    @jax.named_scope("hankel")
    def hankel_of(c):
        ahead = jnp.zeros((LANES, LANES), F32)
        for m in range(total + groups - 2, -1, -1):
            if m < total:
                t, b = m // chunks, m % chunks
                line = windows[t, c : c + 1, LANES * b : LANES * (b + 1)]
                now = pltpu.roll(jnp.broadcast_to(line, (LANES, LANES)), 1, 1, stride=1, stride_axis=0)
            else:
                now = jnp.zeros((LANES, LANES), F32)
            hankel[LANES * c : LANES * (c + 1), LANES * m : LANES * (m + 1)] = jnp.where(
                lanes <= rows, now, ahead
            ).astype(BF)
            ahead = now

    @jax.named_scope("gram")
    def gram_of(t):
        for b in range(chunks):
            flat[t, :, LANES * b : LANES * (b + 1)] = sketch[t, probe_count * b : probe_count * (b + 1), :]
        for g in range(groups):
            some = pl.ds(pl.multiple_of(t * width + LANES * g, LANES), width)
            projected[g] += nt(hankel[:, some], flat[t])
        return nt(flat[t], flat[t])

    for c in range(own // 2):
        hankel_of(c)
    for zo in range(1, n_z):
        arrived(zo, 0, z_send.at[zo], z_recv.at[zo], core)
        for ro in range(1, n_tr):
            go(across(zo, ro))
        go(to_sibling(zo, 0))
    for c in range(own // 2, own):
        hankel_of(c)
    projected[...] = jnp.zeros(projected.shape, F32)
    gram = jnp.zeros((probe_count, probe_count), F32)
    for zo in range(n_z):
        for ro in range(1, n_tr):
            arrived(zo, ro, x_send.at[zo, ro], x_recv.at[zo, ro], core)
            go(to_sibling(zo, ro))
        gram = gram + gram_of(lax.rem(z + n_z - zo, n_z) * 2 + core)
    for zo in range(n_z):
        for ro in range(n_tr):
            arrived(zo, ro, c_send.at[zo, ro], c_recv.at[zo, ro], 1 - core)
        gram = gram + gram_of(lax.rem(z + n_z - zo, n_z) * 2 + 1 - core)

    with jax.named_scope("inverse_factor"):
        inverse = inverse_factor(gram)
        splits = jnp.concatenate(split3(inverse), axis=0)
    with jax.named_scope("basis"):
        for g in range(groups):
            rows_g = slice(probe_count * g, probe_count * (g + 1))
            if g:
                spread[rows_g, : LANES * g] = jnp.zeros((probe_count, LANES * g), BF)
        for t in range(n_tm):
            product = nn(splits, flat[t])
            hi, mid, low = (product[probe_count * i : probe_count * (i + 1)] for i in range(3))
            basis = (low + mid + hi).astype(BF)
            for g in range(groups):
                spread[probe_count * g : probe_count * (g + 1), width * t + LANES * g : width * (t + 1) + LANES * g] = basis
    with jax.named_scope("coefs"):
        coefs = jnp.concatenate([nt(projected[g], inverse, lax.Precision.HIGHEST) for g in range(groups)], axis=1).astype(BF)
        flip = jnp.where(lanes + rows == LANES - 1, 1.0, 0.0).astype(BF)
        coefs = jnp.concatenate(
            [nn(flip, coefs[LANES * c : LANES * (c + 1)]).astype(BF) for c in range(own)], axis=0
        )
    with jax.named_scope("antidiagonals"):
        carry = [jnp.zeros((SUB, LANES), F32) for _ in range(own)]
        for t in range(n_tm):
            product = nn(coefs, spread[:, width * t : width * (t + 1)])
            for c in range(own):
                for b in range(chunks):
                    block = product[LANES * c : LANES * (c + 1), LANES * b : LANES * (b + 1)]
                    turned = pltpu.roll(block, 0, 1, stride=1, stride_axis=0)
                    inside = jnp.where(lanes >= rows, turned, 0.0)
                    beyond = turned - inside
                    near = carry[c]
                    far = jnp.zeros((SUB, LANES), F32)
                    for a in range(LANES // SUB):
                        near = near + inside[SUB * a : SUB * (a + 1)]
                        far = far + beyond[SUB * a : SUB * (a + 1)]
                    carry[c] = far
                    est_out[t, c : c + 1, LANES * b : LANES * (b + 1)] = jnp.sum(near, axis=0, keepdims=True)

    for off in range(1, n_tm):
        dst = lax.rem(tm + off, n_tm)
        go(copy(est_out.at[dst], est_in.at[tm], est_send.at[off], est_recv.at[off], tm=dst))
    est_in[tm] = est_out[tm]
    for off in range(1, n_tm):
        src = lax.rem(tm + n_tm - off, n_tm)
        copy(est_out.at[src], est_in.at[src], est_send.at[off], est_recv.at[off], tm=src).wait_recv()
    for i in range(n_tm):
        out[own * i : own * (i + 1), :] = est_in[i]
    for c in pending:
        c.wait_send()


def on_device(observed, sampled, probes):
    n_tm, n_tr = lax.axis_size("tm"), lax.axis_size("trace")
    taps, traces, count = probes.shape
    width = observed.shape[1]
    groups = taps // LANES
    chunks = width // LANES
    total = n_tm * chunks
    own = traces // n_tm
    n_z = n_tm // 2
    probes = probes.reshape(groups, LANES * traces, count)
    vmem = pl.BlockSpec(memory_space=pltpu.VMEM)
    dma = pltpu.SemaphoreType.DMA
    summed = pl.pallas_call(
        functools.partial(kernel, n_tm, n_tr),
        out_shape=pltpu.VMEM((traces, width), F32),
        in_specs=[vmem, vmem, pl.BlockSpec(memory_space=pl.ANY)],
        out_specs=vmem,
        scratch_shapes=[
            pltpu.VMEM(probes.shape, BF), dma,
            pltpu.VMEM((traces, width), BF),
            pltpu.VMEM((traces, taps), BF),
            pltpu.VMEM((n_tm, own, width), F32),
            pltpu.VMEM((n_tm, own, width), F32),
            pltpu.VMEM((LANES * traces, width + taps - LANES), BF),
            pltpu.VMEM((groups * count, LANES * traces), BF),
            pltpu.VMEM((chunks * count, LANES), BF),
            pltpu.VMEM((n_tr, chunks * count // n_tr, LANES), BF),
            pltpu.VMEM((n_tm, chunks * count, LANES), BF),
            pltpu.VMEM((n_tm, count, width), BF),
            pltpu.VMEM((own * LANES, (total + groups - 1) * LANES), BF),
            pltpu.VMEM((groups * count, (total + groups - 1) * LANES), BF),
            pltpu.VMEM((groups, own * LANES, count), F32),
            pltpu.VMEM((n_tm, own, width), F32),
            pltpu.VMEM((n_tm, own, width), F32),
            dma((2,)),
            dma((n_tm,)), dma((n_tm,)),
            dma((n_tr,)), dma((n_tr,)),
            dma((n_z,)), dma((n_z,)),
            dma((n_z, n_tr)), dma((n_z, n_tr)),
            dma((n_z, n_tr)), dma((n_z, n_tr)),
            dma((n_tm,)), dma((n_tm,)),
        ],
        compiler_params=pltpu.CompilerParams(
            collective_id=0, has_side_effects=True, vmem_limit_bytes=56 * 1024 * 1024
        ),
        cost_estimate=pl.CostEstimate(flops=2 * 10**9, bytes_accessed=2 * 10**6, transcendentals=0),
    )(observed, sampled, probes)
    position = lax.axis_index("tm") * width + jnp.arange(width, dtype=jnp.int32)
    counts = jnp.minimum(position + 1, taps).astype(F32)
    return jnp.where(sampled == 1, observed.astype(F32), summed / counts[None, :])


def solution(mesh):
    in_specs = (P("trace", "tm"), P("trace", "tm"), P(None, "trace", None))
    out_specs = P("trace", "tm")
    return jax.shard_map(
        on_device, mesh=mesh, in_specs=in_specs, out_specs=out_specs, check_vma=False
    )
```

```python
import functools

import jax
import jax.numpy as jnp
from jax import lax
from jax.experimental import pallas as pl
from jax.experimental.pallas import tpu as pltpu
from jax.sharding import PartitionSpec as P

LANES = 128
SUB = 8
BF = jnp.bfloat16
F32 = jnp.float32


def nt(a, b, precision=None):
    return lax.dot_general(a, b, (((1,), (1,)), ((), ())), precision=precision, preferred_element_type=F32)


def nn(a, b):
    return lax.dot_general(a, b, (((1,), (0,)), ((), ())), preferred_element_type=F32)


def split3(x):
    hi = x.astype(BF)
    rest = x - hi.astype(F32)
    mid = rest.astype(BF)
    low = (rest - mid.astype(F32)).astype(BF)
    return hi, mid, low


def inverse_factor(gram):
    size = gram.shape[0]
    blocks = size // SUB
    full_rows = lax.broadcasted_iota(jnp.int32, (size, size), 0)
    full_lanes = lax.broadcasted_iota(jnp.int32, (size, size), 1)
    diagonal = jnp.where(full_rows == full_lanes, gram, 0.0)
    by_row = lax.rsqrt(jnp.sum(diagonal, axis=1, keepdims=True))
    by_lane = lax.rsqrt(jnp.sum(diagonal, axis=0, keepdims=True))
    gram = gram * by_row * by_lane
    rows = lax.broadcasted_iota(jnp.int32, (SUB, size), 0)
    lanes = lax.broadcasted_iota(jnp.int32, (SUB, size), 1)
    left = [gram[SUB * a : SUB * (a + 1)] for a in range(blocks)]
    right = [jnp.where(lanes == rows + SUB * a, 1.0, 0.0).astype(F32) for a in range(blocks)]
    found = []

    def at(x, s):
        return jnp.broadcast_to(x[s : s + 1], (SUB, size))

    for a0 in range(blocks):
        columns = {
            a: [jnp.broadcast_to(left[a][:, SUB * a0 + q : SUB * a0 + q + 1], (SUB, size)) for q in range(SUB)]
            for a in range(a0, blocks)
        }
        wide = columns.pop(a0)
        panel = {"left": left[a0], "right": right[a0]}
        taken = jnp.zeros((SUB, size), F32)
        scale = jnp.ones((SUB, size), F32)
        for s in range(0, SUB, 2):
            first, second = wide[s], wide[s + 1]
            p, q, r = at(first, s), at(first, s + 1), at(second, s + 1)
            det = p * r - q * q
            inverse = 1.0 / det
            here = (rows == s) | (rows == s + 1)
            f0, f1 = jnp.where(here, 0.0, first), jnp.where(here, 0.0, second)

            def eliminate(x):
                x0, x1 = at(x, s), at(x, s + 1)
                y0 = (r * x0 - q * x1) * inverse
                y1 = (p * x1 - q * x0) * inverse
                rest = jnp.where(rows == s, y0, jnp.where(rows == s + 1, y1, x))
                return rest - (f0 * y0 + f1 * y1)

            x0, x1 = at(panel["right"], s), at(panel["right"], s + 1)
            taken = jnp.where(rows == s, x0, jnp.where(rows == s + 1, x1 - (q / p) * x0, taken))
            scale = jnp.where(rows == s, p, jnp.where(rows == s + 1, det / p, scale))
            for k in range(s + 2, SUB):
                wide[k] = eliminate(wide[k])
            panel = {side: eliminate(x) for side, x in panel.items()}
        found.append(taken * lax.rsqrt(scale))
        solved_left = [at(panel["left"], s) for s in range(SUB)]
        solved_right = [at(panel["right"], s) for s in range(SUB)]
        for a in range(a0 + 1, blocks):
            for q in range(SUB):
                left[a] = left[a] - columns[a][q] * solved_left[q]
                right[a] = right[a] - columns[a][q] * solved_right[q]
    return jnp.concatenate(found, axis=0) * by_lane


def kernel(
    n_tm, n_tr,
    observed, sampled, probes_in, out,
    probes, probes_sem, data, halo, slices, windows, rolled, probes_t, part, parts_in, sketch, flat,
    hankel, spread, products, est_out, est_in,
    halo_sems, win_send, win_recv, part_send, part_recv,
    z_send, z_recv, x_send, x_recv, c_send, c_recv, est_send, est_recv,
):
    tm = lax.axis_index("tm")
    tr = lax.axis_index("trace")
    n_z = n_tm // 2
    z = tm // 2
    core = lax.rem(tm, 2)
    traces, width = data.shape
    own = traces // n_tm
    groups, contract, probe_count = probes.shape
    fetch = pltpu.make_async_copy(probes_in, probes, probes_sem)
    fetch.start()
    taps = groups * LANES
    chunks = width // LANES
    total = n_tm * chunks
    samples = n_tm * width
    share = part.shape[0] // n_tr

    def copy(src, dst, send, recv, **to):
        return pltpu.make_async_remote_copy(
            src_ref=src, dst_ref=dst, send_sem=send, recv_sem=recv,
            device_id=to, device_id_type=pl.DeviceIdType.MESH,
        )

    barrier = pltpu.get_barrier_semaphore()
    for off in range(1, n_tm):
        pl.semaphore_signal(barrier, inc=1, device_id={"tm": lax.rem(tm + off, n_tm)}, device_id_type=pl.DeviceIdType.MESH)
    for off in range(1, n_tr):
        pl.semaphore_signal(barrier, inc=1, device_id={"trace": lax.rem(tr + off, n_tr)}, device_id_type=pl.DeviceIdType.MESH)

    masked = jnp.where(sampled[...] == 1, observed[...].astype(F32), 0.0)
    data[...] = masked.astype(BF)
    for i in range(n_tm):
        slices[i] = masked[own * i : own * (i + 1)]
    fetch.wait()
    with jax.named_scope("probes_transposed"):
        for g in range(groups):
            probes_t[probe_count * g : probe_count * (g + 1), :] = probes[g].T
    pl.semaphore_wait(barrier, n_tm + n_tr - 2)

    pending = []
    before = lax.rem(tm + n_tm - 1, n_tm)
    halo_copy = copy(data.at[:, pl.ds(0, taps)], halo, halo_sems.at[0], halo_sems.at[1], tm=before)
    halo_copy.start()
    pending.append(halo_copy)
    for off in range(1, n_tm):
        dst = lax.rem(tm + off, n_tm)
        c = copy(slices.at[dst], windows.at[tm], win_send.at[off], win_recv.at[off], tm=dst)
        c.start()
        pending.append(c)
    windows[tm] = slices[tm]

    def shifted(extended, to):
        reach, keep = extended.shape[1], extended.shape[1] - LANES
        result = jnp.zeros((groups * probe_count, keep), F32)
        step = LANES // 4
        for first in range(0, LANES, step):
            for j in range(first, first + step):
                moved = pltpu.roll(extended, reach - j, 1) if j else extended
                rolled[traces * j : traces * (j + 1), to : to + keep] = moved[:, :keep].astype(BF)
            some = slice(traces * first, traces * (first + step))
            result = result + nn(probes_t[:, some], rolled[some, to : to + keep])
        return result

    nothing = jnp.zeros((traces, LANES), F32)
    with jax.named_scope("sketch_part"):
        inner = shifted(jnp.concatenate([masked, nothing], axis=1), 0)
    halo_copy.wait_recv()
    with jax.named_scope("sketch_part"):
        tail = jnp.where(tm < n_tm - 1, halo[...].astype(F32), 0.0)
        outer = shifted(jnp.concatenate([nothing, tail], axis=1), width)
        for b in range(chunks):
            block = jnp.zeros((probe_count, LANES), F32)
            for g in range(groups):
                mine = slice(probe_count * g, probe_count * (g + 1))
                m, h = b + g, b + g - (chunks - 1)
                if m < chunks:
                    block = block + inner[mine, LANES * m : LANES * (m + 1)]
                if h >= 0:
                    block = block + outer[mine, LANES * h : LANES * (h + 1)]
            part[probe_count * b : probe_count * (b + 1), :] = block.astype(BF)

    for off in range(1, n_tr):
        dst = lax.rem(tr + off, n_tr)
        c = copy(
            part.at[pl.ds(pl.multiple_of(dst * share, share), share), :], parts_in.at[tr],
            part_send.at[off], part_recv.at[off], trace=dst,
        )
        c.start()
        pending.append(c)
    summed = part[pl.ds(pl.multiple_of(tr * share, share), share), :].astype(F32)
    for off in range(1, n_tr):
        src = lax.rem(tr + n_tr - off, n_tr)
        copy(
            part.at[pl.ds(0, share), :], parts_in.at[src], part_send.at[off], part_recv.at[off], trace=src
        ).wait_recv()
        summed = summed + parts_in[src].astype(F32)
    sketch[tm, pl.ds(pl.multiple_of(tr * share, share), share), :] = summed.astype(BF)

    def place(zo, ro, parity):
        t = lax.rem(z + n_z - zo, n_z) * 2 + parity
        r = lax.rem(tr + n_tr - ro, n_tr)
        return sketch.at[t, pl.ds(pl.multiple_of(r * share, share), share), :]

    def along_z(zo):
        here = place(0, 0, core)
        return copy(here, here, z_send.at[zo], z_recv.at[zo], tm=lax.rem(z + zo, n_z) * 2 + core)

    def across(zo, ro):
        here = place(zo, 0, core)
        return copy(here, here, x_send.at[zo, ro], x_recv.at[zo, ro], trace=lax.rem(tr + ro, n_tr))

    def to_sibling(zo, ro):
        here = place(zo, ro, core)
        return copy(here, here, c_send.at[zo, ro], c_recv.at[zo, ro], tm=z * 2 + 1 - core)

    def go(c):
        c.start()
        pending.append(c)

    def arrived(zo, ro, send, recv, parity):
        there = place(zo, ro, parity)
        copy(there, there, send, recv, tm=z * 2 + 1 - core).wait_recv()

    for zo in range(1, n_z):
        go(along_z(zo))
    for ro in range(1, n_tr):
        go(across(0, ro))
    go(to_sibling(0, 0))

    for off in range(1, n_tm):
        src = lax.rem(tm + n_tm - off, n_tm)
        copy(slices.at[src], windows.at[src], win_send.at[off], win_recv.at[off], tm=src).wait_recv()
    rows = lax.broadcasted_iota(jnp.int32, (LANES, LANES), 0)
    lanes = lax.broadcasted_iota(jnp.int32, (LANES, LANES), 1)

    @jax.named_scope("hankel")
    def hankel_of(c):
        ahead = jnp.zeros((LANES, LANES), F32)
        for m in range(total + groups - 2, -1, -1):
            if m < total:
                t, b = m // chunks, m % chunks
                line = windows[t, c : c + 1, LANES * b : LANES * (b + 1)]
                now = pltpu.roll(jnp.broadcast_to(line, (LANES, LANES)), 1, 1, stride=1, stride_axis=0)
            else:
                now = jnp.zeros((LANES, LANES), F32)
            hankel[LANES * c : LANES * (c + 1), LANES * m : LANES * (m + 1)] = jnp.where(
                lanes <= rows, now, ahead
            ).astype(BF)
            ahead = now

    @jax.named_scope("gram")
    def gram_of(t):
        for b in range(chunks):
            flat[t, :, LANES * b : LANES * (b + 1)] = sketch[t, probe_count * b : probe_count * (b + 1), :]
        starts = [pl.multiple_of(t * width + LANES * g, LANES) for g in range(groups)]
        stack = [hankel[:, pl.ds(start, width)] for start in starts] + [flat[t]]
        products[...] += nt(jnp.concatenate(stack, axis=0), flat[t])

    for c in range(own // 2):
        hankel_of(c)
    for zo in range(1, n_z):
        arrived(zo, 0, z_send.at[zo], z_recv.at[zo], core)
        for ro in range(1, n_tr):
            go(across(zo, ro))
        go(to_sibling(zo, 0))
    for c in range(own // 2, own):
        hankel_of(c)
    products[...] = jnp.zeros(products.shape, F32)
    for zo in range(n_z):
        for ro in range(1, n_tr):
            arrived(zo, ro, x_send.at[zo, ro], x_recv.at[zo, ro], core)
            go(to_sibling(zo, ro))
        gram_of(lax.rem(z + n_z - zo, n_z) * 2 + core)
    for zo in range(n_z):
        for ro in range(n_tr):
            arrived(zo, ro, c_send.at[zo, ro], c_recv.at[zo, ro], 1 - core)
        gram_of(lax.rem(z + n_z - zo, n_z) * 2 + 1 - core)

    with jax.named_scope("inverse_factor"):
        inverse = inverse_factor(products[own * groups * LANES :, :])
        splits = jnp.concatenate(split3(inverse), axis=0)
    with jax.named_scope("basis"):
        for g in range(groups):
            rows_g = slice(probe_count * g, probe_count * (g + 1))
            if g:
                spread[rows_g, : LANES * g] = jnp.zeros((probe_count, LANES * g), BF)
        for t in range(n_tm):
            product = nn(splits, flat[t])
            hi, mid, low = (product[probe_count * i : probe_count * (i + 1)] for i in range(3))
            basis = (low + mid + hi).astype(BF)
            for g in range(groups):
                spread[probe_count * g : probe_count * (g + 1), width * t + LANES * g : width * (t + 1) + LANES * g] = basis
    with jax.named_scope("coefs"):
        coefs = jnp.concatenate([nt(products[own * LANES * g : own * LANES * (g + 1), :], inverse, lax.Precision.HIGHEST) for g in range(groups)], axis=1).astype(BF)
        flip = jnp.where(lanes + rows == LANES - 1, 1.0, 0.0).astype(BF)
        coefs = jnp.concatenate(
            [nn(flip, coefs[LANES * c : LANES * (c + 1)]).astype(BF) for c in range(own)], axis=0
        )
    with jax.named_scope("antidiagonals"):
        carry = [jnp.zeros((SUB, LANES), F32) for _ in range(own)]
        for t in range(n_tm):
            product = nn(coefs, spread[:, width * t : width * (t + 1)])
            for c in range(own):
                for b in range(chunks):
                    block = product[LANES * c : LANES * (c + 1), LANES * b : LANES * (b + 1)]
                    turned = pltpu.roll(block, 0, 1, stride=1, stride_axis=0)
                    inside = jnp.where(lanes >= rows, turned, 0.0)
                    beyond = turned - inside
                    near = carry[c]
                    far = jnp.zeros((SUB, LANES), F32)
                    for a in range(LANES // SUB):
                        near = near + inside[SUB * a : SUB * (a + 1)]
                        far = far + beyond[SUB * a : SUB * (a + 1)]
                    carry[c] = far
                    est_out[t, c : c + 1, LANES * b : LANES * (b + 1)] = jnp.sum(near, axis=0, keepdims=True)

    for off in range(1, n_tm):
        dst = lax.rem(tm + off, n_tm)
        go(copy(est_out.at[dst], est_in.at[tm], est_send.at[off], est_recv.at[off], tm=dst))
    est_in[tm] = est_out[tm]
    for off in range(1, n_tm):
        src = lax.rem(tm + n_tm - off, n_tm)
        copy(est_out.at[src], est_in.at[src], est_send.at[off], est_recv.at[off], tm=src).wait_recv()
    for i in range(n_tm):
        out[own * i : own * (i + 1), :] = est_in[i]
    for c in pending:
        c.wait_send()


def on_device(observed, sampled, probes):
    n_tm, n_tr = lax.axis_size("tm"), lax.axis_size("trace")
    taps, traces, count = probes.shape
    width = observed.shape[1]
    groups = taps // LANES
    chunks = width // LANES
    total = n_tm * chunks
    own = traces // n_tm
    n_z = n_tm // 2
    probes = probes.reshape(groups, LANES * traces, count)
    vmem = pl.BlockSpec(memory_space=pltpu.VMEM)
    dma = pltpu.SemaphoreType.DMA
    summed = pl.pallas_call(
        functools.partial(kernel, n_tm, n_tr),
        out_shape=pltpu.VMEM((traces, width), F32),
        in_specs=[vmem, vmem, pl.BlockSpec(memory_space=pl.ANY)],
        out_specs=vmem,
        scratch_shapes=[
            pltpu.VMEM(probes.shape, BF), dma,
            pltpu.VMEM((traces, width), BF),
            pltpu.VMEM((traces, taps), BF),
            pltpu.VMEM((n_tm, own, width), F32),
            pltpu.VMEM((n_tm, own, width), F32),
            pltpu.VMEM((LANES * traces, width + taps), BF),
            pltpu.VMEM((groups * count, LANES * traces), BF),
            pltpu.VMEM((chunks * count, LANES), BF),
            pltpu.VMEM((n_tr, chunks * count // n_tr, LANES), BF),
            pltpu.VMEM((n_tm, chunks * count, LANES), BF),
            pltpu.VMEM((n_tm, count, width), BF),
            pltpu.VMEM((own * LANES, (total + groups - 1) * LANES), BF),
            pltpu.VMEM((groups * count, (total + groups - 1) * LANES), BF),
            pltpu.VMEM((own * groups * LANES + count, count), F32),
            pltpu.VMEM((n_tm, own, width), F32),
            pltpu.VMEM((n_tm, own, width), F32),
            dma((2,)),
            dma((n_tm,)), dma((n_tm,)),
            dma((n_tr,)), dma((n_tr,)),
            dma((n_z,)), dma((n_z,)),
            dma((n_z, n_tr)), dma((n_z, n_tr)),
            dma((n_z, n_tr)), dma((n_z, n_tr)),
            dma((n_tm,)), dma((n_tm,)),
        ],
        compiler_params=pltpu.CompilerParams(
            collective_id=0, has_side_effects=True, vmem_limit_bytes=56 * 1024 * 1024
        ),
        cost_estimate=pl.CostEstimate(flops=2 * 10**9, bytes_accessed=2 * 10**6, transcendentals=0),
    )(observed, sampled, probes)
    position = lax.axis_index("tm") * width + jnp.arange(width, dtype=jnp.int32)
    counts = jnp.minimum(position + 1, taps).astype(F32)
    return jnp.where(sampled == 1, observed.astype(F32), summed / counts[None, :])


def solution(mesh):
    in_specs = (P("trace", "tm"), P("trace", "tm"), P(None, "trace", None))
    out_specs = P("trace", "tm")
    return jax.shard_map(
        on_device, mesh=mesh, in_specs=in_specs, out_specs=out_specs, check_vma=False
    )
```

```python
import functools

import jax
import jax.numpy as jnp
from jax import lax
from jax.experimental import pallas as pl
from jax.experimental.pallas import tpu as pltpu
from jax.sharding import PartitionSpec as P

LANES = 128
SUB = 8
BF = jnp.bfloat16
F32 = jnp.float32


def nt(a, b, precision=None):
    return lax.dot_general(a, b, (((1,), (1,)), ((), ())), precision=precision, preferred_element_type=F32)


def nn(a, b):
    return lax.dot_general(a, b, (((1,), (0,)), ((), ())), preferred_element_type=F32)


def split3(x):
    hi = x.astype(BF)
    rest = x - hi.astype(F32)
    mid = rest.astype(BF)
    low = (rest - mid.astype(F32)).astype(BF)
    return hi, mid, low


def inverse_factor(gram):
    size = gram.shape[0]
    blocks = size // SUB
    full_rows = lax.broadcasted_iota(jnp.int32, (size, size), 0)
    full_lanes = lax.broadcasted_iota(jnp.int32, (size, size), 1)
    diagonal = jnp.where(full_rows == full_lanes, gram, 0.0)
    by_row = lax.rsqrt(jnp.sum(diagonal, axis=1, keepdims=True))
    by_lane = lax.rsqrt(jnp.sum(diagonal, axis=0, keepdims=True))
    gram = gram * by_row * by_lane
    rows = lax.broadcasted_iota(jnp.int32, (SUB, size), 0)
    lanes = lax.broadcasted_iota(jnp.int32, (SUB, size), 1)
    left = [gram[SUB * a : SUB * (a + 1)] for a in range(blocks)]
    right = [jnp.where(lanes == rows + SUB * a, 1.0, 0.0).astype(F32) for a in range(blocks)]
    found = []

    def at(x, s):
        return jnp.broadcast_to(x[s : s + 1], (SUB, size))

    for a0 in range(blocks):
        columns = {
            a: [jnp.broadcast_to(left[a][:, SUB * a0 + q : SUB * a0 + q + 1], (SUB, size)) for q in range(SUB)]
            for a in range(a0, blocks)
        }
        wide = columns.pop(a0)
        panel = {"left": left[a0], "right": right[a0]}
        taken = jnp.zeros((SUB, size), F32)
        scale = jnp.ones((SUB, size), F32)
        for s in range(0, SUB, 2):
            first, second = wide[s], wide[s + 1]
            p, q, r = at(first, s), at(first, s + 1), at(second, s + 1)
            det = p * r - q * q
            inverse = 1.0 / det
            here = (rows == s) | (rows == s + 1)
            f0, f1 = jnp.where(here, 0.0, first), jnp.where(here, 0.0, second)

            def eliminate(x):
                x0, x1 = at(x, s), at(x, s + 1)
                y0 = (r * x0 - q * x1) * inverse
                y1 = (p * x1 - q * x0) * inverse
                rest = jnp.where(rows == s, y0, jnp.where(rows == s + 1, y1, x))
                return rest - (f0 * y0 + f1 * y1)

            x0, x1 = at(panel["right"], s), at(panel["right"], s + 1)
            taken = jnp.where(rows == s, x0, jnp.where(rows == s + 1, x1 - (q / p) * x0, taken))
            scale = jnp.where(rows == s, p, jnp.where(rows == s + 1, det / p, scale))
            for k in range(s + 2, SUB):
                wide[k] = eliminate(wide[k])
            panel = {side: eliminate(x) for side, x in panel.items()}
        found.append(taken * lax.rsqrt(scale))
        solved_left = [at(panel["left"], s) for s in range(SUB)]
        solved_right = [at(panel["right"], s) for s in range(SUB)]
        for a in range(a0 + 1, blocks):
            for q in range(SUB):
                left[a] = left[a] - columns[a][q] * solved_left[q]
                right[a] = right[a] - columns[a][q] * solved_right[q]
    return jnp.concatenate(found, axis=0) * by_lane


def kernel(
    n_tm, n_tr,
    observed, sampled, probes_in, out,
    probes, probes_sem, data, halo, slices, windows, rolled, probes_t, part, parts_in, sketch, flat,
    hankel, spread, projected, est_out, est_in,
    halo_sems, win_send, win_recv, part_send, part_recv,
    z_send, z_recv, x_send, x_recv, c_send, c_recv, est_send, est_recv,
):
    tm = lax.axis_index("tm")
    tr = lax.axis_index("trace")
    n_z = n_tm // 2
    z = tm // 2
    core = lax.rem(tm, 2)
    traces, width = data.shape
    own = traces // n_tm
    groups, contract, probe_count = probes.shape
    fetch = pltpu.make_async_copy(probes_in, probes, probes_sem)
    fetch.start()
    taps = groups * LANES
    chunks = width // LANES
    total = n_tm * chunks
    samples = n_tm * width
    share = part.shape[0] // n_tr

    def copy(src, dst, send, recv, **to):
        return pltpu.make_async_remote_copy(
            src_ref=src, dst_ref=dst, send_sem=send, recv_sem=recv,
            device_id=to, device_id_type=pl.DeviceIdType.MESH,
        )

    barrier = pltpu.get_barrier_semaphore()
    for off in range(1, n_tm):
        pl.semaphore_signal(barrier, inc=1, device_id={"tm": lax.rem(tm + off, n_tm)}, device_id_type=pl.DeviceIdType.MESH)
    for off in range(1, n_tr):
        pl.semaphore_signal(barrier, inc=1, device_id={"trace": lax.rem(tr + off, n_tr)}, device_id_type=pl.DeviceIdType.MESH)

    masked = jnp.where(sampled[...] == 1, observed[...].astype(F32), 0.0)
    data[...] = masked.astype(BF)
    for i in range(n_tm):
        slices[i] = masked[own * i : own * (i + 1)]
    fetch.wait()
    with jax.named_scope("probes_transposed"):
        for g in range(groups):
            probes_t[probe_count * g : probe_count * (g + 1), :] = probes[g].T
    pl.semaphore_wait(barrier, n_tm + n_tr - 2)

    pending = []
    before = lax.rem(tm + n_tm - 1, n_tm)
    halo_copy = copy(data.at[:, pl.ds(0, taps)], halo, halo_sems.at[0], halo_sems.at[1], tm=before)
    halo_copy.start()
    pending.append(halo_copy)
    for off in range(1, n_tm):
        dst = lax.rem(tm + off, n_tm)
        c = copy(slices.at[dst], windows.at[tm], win_send.at[off], win_recv.at[off], tm=dst)
        c.start()
        pending.append(c)
    windows[tm] = slices[tm]

    halo_copy.wait_recv()
    with jax.named_scope("sketch_part"):
        tail = jnp.where(tm < n_tm - 1, halo[...].astype(F32), 0.0)
        extended = jnp.concatenate([masked, tail], axis=1)
        reach = extended.shape[1]
        keep = rolled.shape[1]
        both = jnp.zeros((groups * probe_count, keep), F32)
        step = LANES // 4
        for first in range(0, LANES, step):
            for j in range(first, first + step):
                moved = pltpu.roll(extended, reach - j, 1) if j else extended
                rolled[traces * j : traces * (j + 1), :] = moved[:, :keep].astype(BF)
            some = slice(traces * first, traces * (first + step))
            both = both + nn(probes_t[:, some], rolled[some, :])
        for b in range(chunks):
            block = both[:probe_count, LANES * b : LANES * (b + 1)]
            for g in range(1, groups):
                block = block + both[probe_count * g : probe_count * (g + 1), LANES * (b + g) : LANES * (b + g + 1)]
            part[probe_count * b : probe_count * (b + 1), :] = block.astype(BF)

    part_copies = []
    for off in range(1, n_tr):
        dst = lax.rem(tr + off, n_tr)
        c = copy(
            part.at[pl.ds(pl.multiple_of(dst * share, share), share), :], parts_in.at[tr],
            part_send.at[off], part_recv.at[off], trace=dst,
        )
        c.start()
        pending.append(c)
    summed = part[pl.ds(pl.multiple_of(tr * share, share), share), :].astype(F32)
    for off in range(1, n_tr):
        src = lax.rem(tr + n_tr - off, n_tr)
        copy(
            part.at[pl.ds(0, share), :], parts_in.at[src], part_send.at[off], part_recv.at[off], trace=src
        ).wait_recv()
        summed = summed + parts_in[src].astype(F32)
    sketch[tm, pl.ds(pl.multiple_of(tr * share, share), share), :] = summed.astype(BF)

    def place(zo, ro, parity):
        t = lax.rem(z + n_z - zo, n_z) * 2 + parity
        r = lax.rem(tr + n_tr - ro, n_tr)
        return sketch.at[t, pl.ds(pl.multiple_of(r * share, share), share), :]

    def along_z(zo):
        here = place(0, 0, core)
        return copy(here, here, z_send.at[zo], z_recv.at[zo], tm=lax.rem(z + zo, n_z) * 2 + core)

    def across(zo, ro):
        here = place(zo, 0, core)
        return copy(here, here, x_send.at[zo, ro], x_recv.at[zo, ro], trace=lax.rem(tr + ro, n_tr))

    def to_sibling(zo, ro):
        here = place(zo, ro, core)
        return copy(here, here, c_send.at[zo, ro], c_recv.at[zo, ro], tm=z * 2 + 1 - core)

    def go(c):
        c.start()
        pending.append(c)

    def arrived(zo, ro, send, recv, parity):
        there = place(zo, ro, parity)
        copy(there, there, send, recv, tm=z * 2 + 1 - core).wait_recv()

    for zo in range(1, n_z):
        go(along_z(zo))
    for ro in range(1, n_tr):
        go(across(0, ro))
    go(to_sibling(0, 0))

    for off in range(1, n_tm):
        src = lax.rem(tm + n_tm - off, n_tm)
        copy(slices.at[src], windows.at[src], win_send.at[off], win_recv.at[off], tm=src).wait_recv()
    rows = lax.broadcasted_iota(jnp.int32, (LANES, LANES), 0)
    lanes = lax.broadcasted_iota(jnp.int32, (LANES, LANES), 1)

    @jax.named_scope("hankel")
    def hankel_of(c):
        ahead = jnp.zeros((LANES, LANES), F32)
        for m in range(total + groups - 2, -1, -1):
            if m < total:
                t, b = m // chunks, m % chunks
                line = windows[t, c : c + 1, LANES * b : LANES * (b + 1)]
                now = pltpu.roll(jnp.broadcast_to(line, (LANES, LANES)), 1, 1, stride=1, stride_axis=0)
            else:
                now = jnp.zeros((LANES, LANES), F32)
            hankel[LANES * c : LANES * (c + 1), LANES * m : LANES * (m + 1)] = jnp.where(
                lanes <= rows, now, ahead
            ).astype(BF)
            ahead = now

    @jax.named_scope("gram")
    def gram_of(t):
        for b in range(chunks):
            flat[t, :, LANES * b : LANES * (b + 1)] = sketch[t, probe_count * b : probe_count * (b + 1), :]
        for g in range(groups):
            some = pl.ds(pl.multiple_of(t * width + LANES * g, LANES), width)
            projected[g] += nt(hankel[:, some], flat[t])
        return nt(flat[t], flat[t])

    for c in range(own // 2):
        hankel_of(c)
    for zo in range(1, n_z):
        arrived(zo, 0, z_send.at[zo], z_recv.at[zo], core)
        for ro in range(1, n_tr):
            go(across(zo, ro))
        go(to_sibling(zo, 0))
    for c in range(own // 2, own):
        hankel_of(c)
    projected[...] = jnp.zeros(projected.shape, F32)
    gram = jnp.zeros((probe_count, probe_count), F32)
    for zo in range(n_z):
        for ro in range(1, n_tr):
            arrived(zo, ro, x_send.at[zo, ro], x_recv.at[zo, ro], core)
            go(to_sibling(zo, ro))
        gram = gram + gram_of(lax.rem(z + n_z - zo, n_z) * 2 + core)
    for zo in range(n_z):
        for ro in range(n_tr):
            arrived(zo, ro, c_send.at[zo, ro], c_recv.at[zo, ro], 1 - core)
        gram = gram + gram_of(lax.rem(z + n_z - zo, n_z) * 2 + 1 - core)

    with jax.named_scope("inverse_factor"):
        inverse = inverse_factor(gram)
        splits = jnp.concatenate(split3(inverse), axis=0)
    with jax.named_scope("basis"):
        for g in range(groups):
            rows_g = slice(probe_count * g, probe_count * (g + 1))
            if g:
                spread[rows_g, : LANES * g] = jnp.zeros((probe_count, LANES * g), BF)
        for t in range(n_tm):
            product = nn(splits, flat[t])
            hi, mid, low = (product[probe_count * i : probe_count * (i + 1)] for i in range(3))
            basis = (low + mid + hi).astype(BF)
            for g in range(groups):
                spread[probe_count * g : probe_count * (g + 1), width * t + LANES * g : width * (t + 1) + LANES * g] = basis
    with jax.named_scope("coefs"):
        coefs = jnp.concatenate([nt(projected[g], inverse, lax.Precision.HIGHEST) for g in range(groups)], axis=1).astype(BF)
        flip = jnp.where(lanes + rows == LANES - 1, 1.0, 0.0).astype(BF)
        coefs = jnp.concatenate(
            [nn(flip, coefs[LANES * c : LANES * (c + 1)]).astype(BF) for c in range(own)], axis=0
        )
    with jax.named_scope("antidiagonals"):
        carry = [jnp.zeros((SUB, LANES), F32) for _ in range(own)]
        for t in range(n_tm):
            product = nn(coefs, spread[:, width * t : width * (t + 1)])
            for c in range(own):
                for b in range(chunks):
                    block = product[LANES * c : LANES * (c + 1), LANES * b : LANES * (b + 1)]
                    turned = pltpu.roll(block, 0, 1, stride=1, stride_axis=0)
                    inside = jnp.where(lanes >= rows, turned, 0.0)
                    beyond = turned - inside
                    near = carry[c]
                    far = jnp.zeros((SUB, LANES), F32)
                    for a in range(LANES // SUB):
                        near = near + inside[SUB * a : SUB * (a + 1)]
                        far = far + beyond[SUB * a : SUB * (a + 1)]
                    carry[c] = far
                    est_out[t, c : c + 1, LANES * b : LANES * (b + 1)] = jnp.sum(near, axis=0, keepdims=True)

    for off in range(1, n_tm):
        dst = lax.rem(tm + off, n_tm)
        go(copy(est_out.at[dst], est_in.at[tm], est_send.at[off], est_recv.at[off], tm=dst))
    est_in[tm] = est_out[tm]
    for off in range(1, n_tm):
        src = lax.rem(tm + n_tm - off, n_tm)
        copy(est_out.at[src], est_in.at[src], est_send.at[off], est_recv.at[off], tm=src).wait_recv()
    for i in range(n_tm):
        out[own * i : own * (i + 1), :] = est_in[i]
    for c in pending:
        c.wait_send()


def on_device(observed, sampled, probes):
    n_tm, n_tr = lax.axis_size("tm"), lax.axis_size("trace")
    taps, traces, count = probes.shape
    width = observed.shape[1]
    groups = taps // LANES
    chunks = width // LANES
    total = n_tm * chunks
    own = traces // n_tm
    n_z = n_tm // 2
    probes = probes.reshape(groups, LANES * traces, count)
    vmem = pl.BlockSpec(memory_space=pltpu.VMEM)
    dma = pltpu.SemaphoreType.DMA
    summed = pl.pallas_call(
        functools.partial(kernel, n_tm, n_tr),
        out_shape=pltpu.VMEM((traces, width), F32),
        in_specs=[vmem, vmem, pl.BlockSpec(memory_space=pl.ANY)],
        out_specs=vmem,
        scratch_shapes=[
            pltpu.VMEM(probes.shape, BF), dma,
            pltpu.VMEM((traces, width), BF),
            pltpu.VMEM((traces, taps), BF),
            pltpu.VMEM((n_tm, own, width), F32),
            pltpu.VMEM((n_tm, own, width), F32),
            pltpu.VMEM((LANES * traces, width + taps - LANES), BF),
            pltpu.VMEM((groups * count, LANES * traces), BF),
            pltpu.VMEM((chunks * count, LANES), BF),
            pltpu.VMEM((n_tr, chunks * count // n_tr, LANES), BF),
            pltpu.VMEM((n_tm, chunks * count, LANES), BF),
            pltpu.VMEM((n_tm, count, width), BF),
            pltpu.VMEM((own * LANES, (total + groups - 1) * LANES), BF),
            pltpu.VMEM((groups * count, (total + groups - 1) * LANES), BF),
            pltpu.VMEM((groups, own * LANES, count), F32),
            pltpu.VMEM((n_tm, own, width), F32),
            pltpu.VMEM((n_tm, own, width), F32),
            dma((2,)),
            dma((n_tm,)), dma((n_tm,)),
            dma((n_tr,)), dma((n_tr,)),
            dma((n_z,)), dma((n_z,)),
            dma((n_z, n_tr)), dma((n_z, n_tr)),
            dma((n_z, n_tr)), dma((n_z, n_tr)),
            dma((n_tm,)), dma((n_tm,)),
        ],
        compiler_params=pltpu.CompilerParams(
            collective_id=0, has_side_effects=True, vmem_limit_bytes=56 * 1024 * 1024
        ),
        cost_estimate=pl.CostEstimate(flops=2 * 10**9, bytes_accessed=2 * 10**6, transcendentals=0),
    )(observed, sampled, probes)
    position = lax.axis_index("tm") * width + jnp.arange(width, dtype=jnp.int32)
    counts = jnp.minimum(position + 1, taps).astype(F32)
    return jnp.where(sampled == 1, observed.astype(F32), summed / counts[None, :])


def solution(mesh):
    in_specs = (P("trace", "tm"), P("trace", "tm"), P(None, "trace", None))
    out_specs = P("trace", "tm")
    return jax.shard_map(
        on_device, mesh=mesh, in_specs=in_specs, out_specs=out_specs, check_vma=False
    )
```
